32 devices in a mesh: dom: 2 (over x), inst: 16 (over z, y, core).
Axes of the slice: x: 2, y: 2, z: 4, core: 2. Of those that a mesh axis runs over, the one named last changes fastest.
Arguments:
- tokens: bfloat16 [2, 64, 8192], P(None, ('dom', 'inst')), parts along dimension 1, may hold values from -100 to 100
- norm_gain: bfloat16 [8192], replicated, may hold values from 0.099609375 to 1.8984375
- qkv_weight: bfloat16 [10240, 8192], P('inst'), may hold values from -0.0625 to 0.0625
- out_weight: bfloat16 [8192, 8192], P('inst'), may hold values from -0.0625 to 0.0625
- qkv_down: bfloat16 [4, 16, 8192], replicated, may hold values from -0.0625 to 0.0625
- qkv_up: bfloat16 [4, 16, 10240], P(None, None, 'inst'), may hold values from -1.5 to 1.5
- out_down: bfloat16 [4, 16, 8192], replicated, may hold values from -0.0625 to 0.0625
- out_up: bfloat16 [4, 16, 8192], P(None, None, 'inst'), may hold values from -1.5 to 1.5
- adapter_ids: int32 [64], P(('dom', 'inst')), parts along dimension 0, may hold values from 0 to 3
- cached_len: int32 [64], P(('dom', 'inst')), parts along dimension 0, may hold values from 1 to 1024, as said below
- page_table: int32 [64, 64], P(('dom', 'inst')), parts along dimension 0, may hold values from 0 to 127, as said below
- send_slots: int32 [32, 128], P(('dom', 'inst')), parts along dimension 0, may hold values from -1 to 127, as said below
- kv_pool: bfloat16 [4096, 16, 2048], P(('dom', 'inst')), parts along dimension 0, may hold values from -140 to 140
Outputs:
- decoded: bfloat16 [2, 64, 8192], P(None, ('dom', 'inst')), parts along dimension 1
The draws below stay inside these ranges and needn't reach their ends.
There are 2 independent parts, one for each index of `dom`. The reference program is written for one: setup_inputs(seed, part) draws one part's arguments, and reference() takes and returns one part's arrays. A program takes and returns all parts, laid end to end along the dimension named above; an argument that names none is the same for every part. Nothing has to cross between parts.
Inputs may be any that keep to these rules, and one draw needn't show every extreme that they name: `page_table`: for each request, page j's arrival row names a distinct page: the 64 pages of the 2 requests of one instance use every arrival row 0 .. 127 once, so every instance receives 8 pages from every instance, itself included, in an order drawn from the seed. `send_slots`: row src, column d * 8 + c is the slot in src's pool of the page that arrives as row src * 8 + c at instance d, or -1 where that page lies wholly at or beyond its request's cached length; a slot appears at most once in a row. `cached_len`: at least one request has exactly 1024 cached tokens.
All inputs are finite; a program needn't handle non-finite values.
Results may differ from the reference program's by a relative error of at most 0.022.
The reference program's roundings to bfloat16 on the way count: a program that leaves them out, or rounds other values in their place, can miss the bound.
Values may be sent and summed in bfloat16 or wider, within the bound.
A program may use at most 128 MiB of HBM per device.

```python
import math
import jax
import jax.numpy as jnp
from jax import lax

D = 8192
H = 64
KVH = 8
HD = 128
RANK = 16
NA = 4
REQ_DEV = 2
MAXP = 64
PAGE_LEN = 16
STEPS = 2
REQS = 32
PAGES_DEV = 128
CAP = 8
POOL = 2048
QKV = 10240


def migration_plan(key):
    subkeys = jax.random.split(jax.random.fold_in(key, 17), 5)
    inst_count = REQS // REQ_DEV
    full_len = MAXP * PAGE_LEN
    device_top = jax.random.randint(subkeys[0], (inst_count, 1), full_len // 2, full_len + 1)
    spread = jax.random.randint(subkeys[1], (inst_count, REQ_DEV), 0, 1 << 20)
    low_len = device_top // 2
    lengths = low_len + spread % (device_top - low_len + 1)
    chosen = jax.random.randint(subkeys[2], (), 0, inst_count * REQ_DEV)
    flat_index = jnp.arange(inst_count * REQ_DEV).reshape(inst_count, REQ_DEV)
    lengths = jnp.where(flat_index == chosen, full_len, lengths).astype(jnp.int32)
    live_pages = (lengths + PAGE_LEN - 1) // PAGE_LEN
    arrival = jax.vmap(lambda subkey: jax.random.permutation(subkey, PAGES_DEV))(jax.random.split(subkeys[3], inst_count)).astype(jnp.int32)
    storage = jax.vmap(lambda subkey: jax.random.permutation(subkey, PAGES_DEV))(jax.random.split(subkeys[4], inst_count)).astype(jnp.int32)
    inverse = jnp.argsort(arrival, axis=1).astype(jnp.int32)
    by_source = inverse.reshape(inst_count, inst_count, CAP).transpose(1, 0, 2)
    request = by_source // MAXP
    page_slot = by_source % MAXP
    dest_index = jnp.broadcast_to(jnp.arange(inst_count)[None, :, None], request.shape)
    live_count = live_pages[dest_index, request]
    is_live = page_slot < live_count
    pool_slots = jnp.where(is_live, storage.reshape(inst_count, inst_count, CAP), -1)
    return (lengths.reshape(-1), arrival.reshape(inst_count * REQ_DEV, MAXP), pool_slots.reshape(inst_count, PAGES_DEV).astype(jnp.int32))


def draw_cached_len(key, part):
    return migration_plan(key)[0]


def draw_page_table(key, part):
    return migration_plan(key)[1]


def draw_send_slots(key, part):
    return migration_plan(key)[2]


def draw_tokens(key, part):
    key = jax.random.fold_in(key, 3)
    subkeys = jax.random.split(key, 3)
    row_scale = jnp.exp(jax.random.uniform(subkeys[0], (STEPS, REQS, 1), jnp.float32, jnp.log(0.5), jnp.log(5.0)))
    col_scale = jnp.exp(jax.random.uniform(subkeys[1], (1, 1, D), jnp.float32, jnp.log(0.5), jnp.log(5.0)))
    base = jnp.clip(jax.random.normal(subkeys[2], (STEPS, REQS, D), jnp.float32), -3.9, 3.9)
    return (base * row_scale * col_scale).astype(jnp.bfloat16)


def draw_kv_pool(key, part):
    key = jax.random.fold_in(key, 5)
    subkeys = jax.random.split(key, 1)
    shape = (POOL, PAGE_LEN, 2 * KVH * HD)
    base = 2.0 * jnp.clip(jax.random.normal(subkeys[0], shape, jnp.float32), -6.0, 6.0)
    return base.astype(jnp.bfloat16)


def set_ends(result, key, least, largest):
    spot = [jax.random.randint(jax.random.fold_in(key, axis), (), 0, length) for axis, length in enumerate(result.shape)]
    widest = result.shape.index(max(result.shape))
    beside = spot[:widest] + [(spot[widest] + 1) % result.shape[widest]] + spot[widest + 1:]
    return result.at[tuple(spot)].set(least).at[tuple(beside)].set(largest)


def block_scale(rng, dims, shards, smallest, top_value):
    loudness = 1.0
    for axis_at, shards_of in shards:
        steps = jax.random.uniform(jax.random.fold_in(jax.random.fold_in(rng, 6), axis_at), (shards_of,), jnp.float32, smallest / len(shards), top_value / len(shards))
        loudness = loudness * jnp.repeat(jnp.exp(steps), dims[axis_at] // shards_of).reshape((-1,) + (1,) * (len(dims) - 1 - axis_at))
    return loudness


def centred(key, extent, scale, reach, pieces=(), kind=jnp.bfloat16):
    drawn = jax.random.normal(key, extent, jnp.float32) * scale
    if len(pieces) > 0:
        drawn = block_scale(key, extent, pieces, -0.22, 0.18) * drawn
    return jnp.clip(drawn, min=-reach, max=reach).astype(kind)


def setup_inputs(seed: int = 0, part: int = 0) -> dict:
    splits = jax.random.split(jax.random.key(seed), 14)
    part_splits = jax.random.split(jax.random.fold_in(splits[13], part), 14)
    return {
        "tokens": draw_tokens(jax.random.fold_in(jax.random.fold_in(splits[13], part), 71), part),
        "norm_gain": jnp.clip(1.0 + 0.18 * jax.random.normal(splits[1], (D,), jnp.float32), 0.099609375, 1.8984375).astype(jnp.bfloat16),
        "qkv_weight": centred(splits[2], (QKV, D), D ** -0.5, 0.0625, ((0, 16),)),
        "out_weight": centred(splits[3], (D, D), D ** -0.5, 0.0625, ((0, 16),)),
        "qkv_down": centred(splits[4], (NA, RANK, D), D ** -0.5, 0.0625),
        "qkv_up": centred(splits[5], (NA, RANK, QKV), RANK ** -0.5, 1.5, ((2, 16),)),
        "out_down": centred(splits[6], (NA, RANK, D), D ** -0.5, 0.0625),
        "out_up": centred(splits[7], (NA, RANK, D), RANK ** -0.5, 1.5, ((2, 16),)),
        "adapter_ids": set_ends(jax.random.randint(part_splits[8], (REQS,), 0, NA), jax.random.fold_in(part_splits[8], 1), 0, NA - 1).astype(jnp.int32),
        "cached_len": draw_cached_len(jax.random.fold_in(jax.random.fold_in(splits[13], part), 71), part),
        "page_table": draw_page_table(jax.random.fold_in(jax.random.fold_in(splits[13], part), 71), part),
        "send_slots": draw_send_slots(jax.random.fold_in(jax.random.fold_in(splits[13], part), 71), part),
        "kv_pool": draw_kv_pool(jax.random.fold_in(jax.random.fold_in(splits[13], part), 71), part),
    }


EPSILON = 1e-05
ROPE_BASE = 500000.0
MASKED = -1e+30

def rotate(vectors, position):
    half = vectors.shape[-1] // 2
    freqs = ROPE_BASE ** (-(jnp.arange(half, dtype=jnp.float32) * 2.0) / vectors.shape[-1])
    angle = position[:, None, None] * freqs
    cosine = jnp.cos(angle)
    sine = jnp.sin(angle)
    first = vectors[..., :half]
    second = vectors[..., half:]
    return jnp.concatenate([first * cosine - second * sine, second * cosine + first * sine], axis=-1)

def normalize(hidden, norm_gain):
    values = hidden.astype(jnp.float32)
    factor = lax.rsqrt(lax.optimization_barrier(jnp.mean(values * values, axis=-1, keepdims=True)) + EPSILON)
    return (values * factor * norm_gain.astype(jnp.float32)).astype(jnp.bfloat16)

def reference(tokens, norm_gain, qkv_weight, out_weight, qkv_down, qkv_up, out_down, out_up, adapter_ids, cached_len, page_table, send_slots, kv_pool):
    owner_dev = (jnp.arange(REQS) // REQ_DEV).astype(jnp.int32)
    source_dev = (page_table // CAP).astype(jnp.int32)
    source_pos = (page_table % CAP).astype(jnp.int32)
    stored = send_slots[source_dev, owner_dev[:, None] * CAP + source_pos]
    pool_row = (source_dev * PAGES_DEV + jnp.maximum(stored, 0)).astype(jnp.int32)
    ctx_tokens = MAXP * PAGE_LEN
    visible = jnp.arange(ctx_tokens)[None, :] < cached_len[:, None]
    scale = 1.0 / math.sqrt(HD)
    down_rows = qkv_down[adapter_ids].astype(jnp.float32)
    up_rows = qkv_up[adapter_ids].astype(jnp.float32)
    out_down_rows = out_down[adapter_ids].astype(jnp.float32)
    out_up_rows = out_up[adapter_ids].astype(jnp.float32)
    groups = H // KVH

    def attend_one(items):
        query_one, rows_one, visible_one, keys_one, vals_one = items
        pages = kv_pool[rows_one].reshape(ctx_tokens, 2 * KVH * HD)
        cached_keys = pages[:, :KVH * HD].reshape(ctx_tokens, KVH, HD).astype(jnp.float32)
        cached_vals = pages[:, KVH * HD:].reshape(ctx_tokens, KVH, HD).astype(jnp.float32)
        grouped = query_one.astype(jnp.float32).reshape(KVH, groups, HD)
        old_scores = jnp.einsum('kgd,lkd->kgl', grouped, cached_keys) * scale
        old_scores = jnp.where(visible_one[None, None, :], old_scores, MASKED)
        new_scores = jnp.einsum('kgd,nkd->kgn', grouped, keys_one.astype(jnp.float32)) * scale
        top_score = jnp.maximum(lax.optimization_barrier(jnp.max(old_scores, axis=-1)), lax.optimization_barrier(jnp.max(new_scores, axis=-1)))[..., None]
        old_weights = jnp.exp(old_scores - top_score)
        new_weights = jnp.exp(new_scores - top_score)
        total = lax.optimization_barrier(jnp.sum(old_weights, axis=-1)) + lax.optimization_barrier(jnp.sum(new_weights, axis=-1))
        mixed = jnp.einsum('kgl,lkd->kgd', old_weights.astype(jnp.bfloat16).astype(jnp.float32), cached_vals)
        mixed = mixed + jnp.einsum('kgn,nkd->kgd', new_weights.astype(jnp.bfloat16).astype(jnp.float32), vals_one.astype(jnp.float32))
        return (mixed / total[..., None]).reshape(D).astype(jnp.bfloat16)
    new_keys = []
    new_vals = []
    results = []
    for step_idx in range(STEPS):
        normed = normalize(tokens[step_idx], norm_gain)
        low_in = jnp.einsum('td,tkd->tk', normed.astype(jnp.float32), down_rows).astype(jnp.bfloat16)
        projected = jnp.dot(normed, qkv_weight.T, preferred_element_type=jnp.float32)
        projected = (projected + jnp.einsum('tk,tkc->tc', low_in.astype(jnp.float32), up_rows)).astype(jnp.bfloat16)
        position = (cached_len + step_idx).astype(jnp.float32)
        query = rotate(projected[:, :D].astype(jnp.float32).reshape(REQS, H, HD), position).astype(jnp.bfloat16)
        fresh_key = rotate(projected[:, D:D + KVH * HD].astype(jnp.float32).reshape(REQS, KVH, HD), position).astype(jnp.bfloat16)
        fresh_val = projected[:, D + KVH * HD:].reshape(REQS, KVH, HD)
        new_keys.append(fresh_key)
        new_vals.append(fresh_val)
        recent_keys = jnp.stack(new_keys, axis=1)
        recent_vals = jnp.stack(new_vals, axis=1)
        attended = lax.map(attend_one, (query, pool_row, visible, recent_keys, recent_vals))
        low_out = jnp.einsum('td,tkd->tk', attended.astype(jnp.float32), out_down_rows).astype(jnp.bfloat16)
        output = jnp.dot(attended, out_weight.T, preferred_element_type=jnp.float32)
        output = output + jnp.einsum('tk,tkc->tc', low_out.astype(jnp.float32), out_up_rows)
        results.append(output.astype(jnp.bfloat16))
    return jnp.stack(results, axis=0)
```

```python
import functools
import math

import jax
import jax.numpy as jnp
from jax import lax
from jax.sharding import PartitionSpec as P

H = 64
KVH = 8
HD = 128
GROUPS = H // KVH
EXTRA = 128

EPSILON = 1e-05
ROPE_BASE = 500000.0
MASKED = -1e30


def rotate(vectors, position):
    half = vectors.shape[-1] // 2
    freqs = ROPE_BASE ** (-(jnp.arange(half, dtype=jnp.float32) * 2.0) / vectors.shape[-1])
    angle = position[:, None, None] * freqs
    cosine = jnp.cos(angle)
    sine = jnp.sin(angle)
    first = vectors[..., :half]
    second = vectors[..., half:]
    return jnp.concatenate(
        [first * cosine - second * sine, second * cosine + first * sine], axis=-1
    )


def normalize(hidden, norm_gain):
    values = hidden.astype(jnp.float32)
    factor = lax.rsqrt(jnp.mean(values * values, axis=-1, keepdims=True) + EPSILON)
    return (values * factor * norm_gain.astype(jnp.float32)).astype(jnp.bfloat16)


def expand(rows, down_maps, selector):
    every = jnp.einsum("rd,akd->rak", rows, down_maps, preferred_element_type=jnp.float32)
    chosen = jnp.sum(every * selector[:, :, None], axis=1).astype(jnp.bfloat16)
    spread = selector[:, :, None] * chosen[:, None, :].astype(jnp.float32)
    return spread.reshape(rows.shape[0], -1).astype(jnp.bfloat16)


def columns(gathered, spread, weight, up_maps):
    base = lax.dot_general(
        gathered, weight, (((1,), (1,)), ((), ())), preferred_element_type=jnp.float32
    )
    extra = jnp.dot(
        spread, up_maps.reshape(-1, up_maps.shape[2]), preferred_element_type=jnp.float32
    )
    return (base + extra).astype(jnp.bfloat16)


def page_codes(page_table, cached_len, page_len):
    reqs, maxp = page_table.shape
    begins = jnp.arange(maxp, dtype=jnp.int32) * page_len
    valid = jnp.clip(cached_len[:, None] - begins[None, :], 0, page_len)
    code = valid + 32 * jnp.arange(reqs, dtype=jnp.int32)[:, None]
    rows = jnp.arange(reqs * maxp, dtype=jnp.int32)
    match = page_table.reshape(-1)[:, None] == rows[None, :]
    return jnp.sum(jnp.where(match, code.reshape(-1)[:, None], 0), axis=0)


def per_device(
    n,
    tokens,
    norm_gain,
    qkv_weight,
    out_weight,
    qkv_down,
    qkv_up,
    out_down,
    out_up,
    adapter_ids,
    cached_len,
    page_table,
    send_slots,
    kv_pool,
):
    steps, reqs, width = tokens.shape
    adapters, rank = qkv_down.shape[:2]
    half_width = KVH * HD
    page_len = kv_pool.shape[1]
    pages = send_slots.shape[1]
    cap = pages // n
    rows = steps * reqs
    scale = 1.0 / math.sqrt(HD)
    me = lax.axis_index("inst")

    selector = (adapter_ids[:, None] == jnp.arange(adapters)[None, :]).astype(jnp.float32)
    selector = jnp.tile(selector, (steps, 1))
    normed = normalize(tokens, norm_gain).reshape(rows, width)
    spread = expand(normed, qkv_down, selector)
    codes = page_codes(page_table, cached_len, page_len)
    position = jnp.concatenate([cached_len + s for s in range(steps)])
    extra = jnp.concatenate(
        [
            spread,
            codes.reshape(rows, -1).astype(jnp.bfloat16),
            (position // 64).astype(jnp.bfloat16)[:, None],
            (position % 64).astype(jnp.bfloat16)[:, None],
        ],
        axis=1,
    )
    extra = jnp.pad(extra, ((0, 0), (0, EXTRA - extra.shape[1])))
    sent = jnp.concatenate([normed, extra], axis=1)
    everyone = lax.all_gather(sent, "inst", axis=0, tiled=True)
    low = adapters * rank
    per_row = pages // rows
    projected = columns(everyone[:, :width], everyone[:, width : width + low], qkv_weight, qkv_up)
    all_codes = everyone[:, width + low : width + low + per_row].astype(jnp.int32)
    my_codes = lax.dynamic_slice_in_dim(all_codes.reshape(n, pages), me * cap, cap, axis=1)
    spot = everyone[:, width + low + per_row : width + low + per_row + 2].astype(jnp.float32)
    all_position = spot[:, 0] * 64.0 + spot[:, 1]

    gathered = lax.all_gather(projected, "inst", axis=1, tiled=True)
    query = rotate(
        gathered[:, :width].astype(jnp.float32).reshape(n * rows, H, HD), all_position
    ).astype(jnp.bfloat16)
    query = query.reshape(n, rows, KVH, GROUPS, HD).transpose(0, 2, 1, 3, 4)
    query = query.reshape(n, KVH, rows * GROUPS, HD)

    slots = jnp.maximum(send_slots[0], 0)
    context = kv_pool[slots].reshape(n, cap * page_len, 2, KVH, HD)
    keys = context[:, :, 0]
    vals = context[:, :, 1]
    scores = (
        jnp.einsum("dkqf,dtkf->dkqt", query, keys, preferred_element_type=jnp.float32) * scale
    )
    within = jnp.arange(page_len)[None, None, :]
    valid = (within < (my_codes % 32)[:, :, None]).reshape(n, 1, cap * page_len)
    owner = jnp.broadcast_to((my_codes // 32)[:, :, None], (n, cap, page_len)).reshape(n, 1, -1)
    row_req = jnp.tile(jnp.repeat(jnp.arange(reqs), GROUPS), steps)[None, :, None]
    mask = (valid & (owner == row_req))[:, None]
    scores = jnp.where(mask, scores, MASKED)
    top = jnp.max(scores, axis=-1)
    weights = jnp.where(mask, jnp.exp(scores - top[..., None]), 0.0)
    total = jnp.sum(weights, axis=-1)
    mixed = jnp.einsum(
        "dkqt,dtkf->dkqf", weights.astype(jnp.bfloat16), vals, preferred_element_type=jnp.float32
    ).astype(jnp.bfloat16)
    stats = jnp.stack([top, total], axis=1)
    mixed = lax.all_to_all(mixed, "inst", split_axis=0, concat_axis=0, tiled=True)
    stats = lax.all_to_all(stats, "inst", split_axis=0, concat_axis=0, tiled=True)

    mine = lax.dynamic_slice_in_dim(gathered, me * rows, rows, axis=0)
    own_pos = position.astype(jnp.float32)
    own_query = lax.dynamic_index_in_dim(query, me, axis=0, keepdims=False)
    own_query = own_query.reshape(KVH, steps, reqs, GROUPS, HD)
    fresh_key = rotate(
        mine[:, width : width + half_width].astype(jnp.float32).reshape(rows, KVH, HD), own_pos
    ).astype(jnp.bfloat16)
    fresh_key = fresh_key.reshape(steps, reqs, KVH, HD)
    fresh_val = mine[:, width + half_width :].reshape(steps, reqs, KVH, HD)
    new_scores = (
        jnp.einsum("ksrgf,nrkf->ksrgn", own_query, fresh_key, preferred_element_type=jnp.float32)
        * scale
    )
    seen = jnp.arange(steps)[None, :] <= jnp.arange(steps)[:, None]
    seen = seen[None, :, None, None, :]
    new_scores = jnp.where(seen, new_scores, MASKED)
    tops = stats[:, 0].reshape(n, KVH, steps, reqs, GROUPS)
    totals = stats[:, 1].reshape(n, KVH, steps, reqs, GROUPS)
    best = jnp.maximum(jnp.max(tops, axis=0), jnp.max(new_scores, axis=-1))
    factors = jnp.exp(tops - best[None])
    new_weights = jnp.where(seen, jnp.exp(new_scores - best[..., None]), 0.0)
    total = jnp.sum(factors * totals, axis=0) + jnp.sum(new_weights, axis=-1)
    mixed = mixed.reshape(n, KVH, steps, reqs, GROUPS, HD).astype(jnp.float32)
    summed = jnp.sum(mixed * factors[..., None], axis=0)
    summed = summed + jnp.einsum(
        "ksrgn,nrkf->ksrgf",
        new_weights.astype(jnp.bfloat16),
        fresh_val,
        preferred_element_type=jnp.float32,
    )
    attended = (summed / total[..., None]).transpose(1, 2, 0, 3, 4)
    attended = attended.reshape(rows, width).astype(jnp.bfloat16)
    low_out = expand(attended, out_down, selector)
    both = jnp.concatenate([attended, jnp.pad(low_out, ((0, 0), (0, EXTRA - low)))], axis=1)
    every_att = lax.all_gather(both, "inst", axis=0, tiled=True)
    out_cols = columns(every_att[:, :width], every_att[:, width : width + low], out_weight, out_up)
    result = lax.all_to_all(out_cols, "inst", split_axis=0, concat_axis=1, tiled=True)
    return result.reshape(steps, reqs, width)


def solution(mesh):
    in_specs = (
        P(None, ("dom", "inst"), None),
        P(),
        P("inst", None),
        P("inst", None),
        P(),
        P(None, None, "inst"),
        P(),
        P(None, None, "inst"),
        P(("dom", "inst")),
        P(("dom", "inst")),
        P(("dom", "inst"), None),
        P(("dom", "inst"), None),
        P(("dom", "inst"), None, None),
    )
    out_specs = P(None, ("dom", "inst"), None)
    return jax.shard_map(
        functools.partial(per_device, mesh.shape["inst"]),
        mesh=mesh,
        in_specs=in_specs,
        out_specs=out_specs,
        check_vma=False,
    )
```

```python
import functools
import math

import jax
import jax.numpy as jnp
from jax import lax
from jax.experimental import pallas as pl
from jax.experimental.pallas import tpu as pltpu
from jax.sharding import PartitionSpec as P

H = 64
KVH = 8
HD = 128
GROUPS = H // KVH
EXTRA = 128

EPSILON = 1e-05
ROPE_BASE = 500000.0
MASKED = -1e30


def rotate(vectors, position):
    half = vectors.shape[-1] // 2
    freqs = ROPE_BASE ** (-(jnp.arange(half, dtype=jnp.float32) * 2.0) / vectors.shape[-1])
    angle = position[:, None, None] * freqs
    cosine = jnp.cos(angle)
    sine = jnp.sin(angle)
    first = vectors[..., :half]
    second = vectors[..., half:]
    return jnp.concatenate(
        [first * cosine - second * sine, second * cosine + first * sine], axis=-1
    )


def normalize(hidden, norm_gain):
    values = hidden.astype(jnp.float32)
    factor = lax.rsqrt(jnp.mean(values * values, axis=-1, keepdims=True) + EPSILON)
    return (values * factor * norm_gain.astype(jnp.float32)).astype(jnp.bfloat16)


def expand(rows, down_maps, selector):
    every = jnp.einsum("rd,akd->rak", rows, down_maps, preferred_element_type=jnp.float32)
    chosen = jnp.sum(every * selector[:, :, None], axis=1).astype(jnp.bfloat16)
    spread = selector[:, :, None] * chosen[:, None, :].astype(jnp.float32)
    return spread.reshape(rows.shape[0], -1).astype(jnp.bfloat16)


def columns(gathered, spread, weight, up_maps):
    base = lax.dot_general(
        gathered, weight, (((1,), (1,)), ((), ())), preferred_element_type=jnp.float32
    )
    extra = jnp.dot(
        spread, up_maps.reshape(-1, up_maps.shape[2]), preferred_element_type=jnp.float32
    )
    return (base + extra).astype(jnp.bfloat16)


def page_codes(page_table, cached_len, page_len):
    reqs, maxp = page_table.shape
    begins = jnp.arange(maxp, dtype=jnp.int32) * page_len
    valid = jnp.clip(cached_len[:, None] - begins[None, :], 0, page_len)
    code = valid + 32 * jnp.arange(reqs, dtype=jnp.int32)[:, None]
    rows = jnp.arange(reqs * maxp, dtype=jnp.int32)
    match = page_table.reshape(-1)[:, None] == rows[None, :]
    return jnp.sum(jnp.where(match, code.reshape(-1)[:, None], 0), axis=0)


def per_device(
    n,
    tokens,
    norm_gain,
    qkv_weight,
    out_weight,
    qkv_down,
    qkv_up,
    out_down,
    out_up,
    adapter_ids,
    cached_len,
    page_table,
    send_slots,
    kv_pool,
):
    steps, reqs, width = tokens.shape
    adapters, rank = qkv_down.shape[:2]
    half_width = KVH * HD
    page_len = kv_pool.shape[1]
    pages = send_slots.shape[1]
    cap = pages // n
    rows = steps * reqs
    scale = 1.0 / math.sqrt(HD)
    me = lax.axis_index("inst")

    selector = (adapter_ids[:, None] == jnp.arange(adapters)[None, :]).astype(jnp.float32)
    selector = jnp.tile(selector, (steps, 1))
    normed = normalize(tokens, norm_gain).reshape(rows, width)
    spread = expand(normed, qkv_down, selector)
    codes = page_codes(page_table, cached_len, page_len)
    position = jnp.concatenate([cached_len + s for s in range(steps)])
    extra = jnp.concatenate(
        [
            spread,
            codes.reshape(rows, -1).astype(jnp.bfloat16),
            (position // 64).astype(jnp.bfloat16)[:, None],
            (position % 64).astype(jnp.bfloat16)[:, None],
        ],
        axis=1,
    )
    extra = jnp.pad(extra, ((0, 0), (0, EXTRA - extra.shape[1])))
    sent = jnp.concatenate([normed, extra], axis=1)
    everyone = lax.all_gather(sent, "inst", axis=0, tiled=True)
    low = adapters * rank
    per_row = pages // rows
    projected = columns(everyone[:, :width], everyone[:, width : width + low], qkv_weight, qkv_up)
    all_codes = everyone[:, width + low : width + low + per_row].astype(jnp.int32)
    my_codes = lax.dynamic_slice_in_dim(all_codes.reshape(n, pages), me * cap, cap, axis=1)
    spot = everyone[:, width + low + per_row : width + low + per_row + 2].astype(jnp.float32)
    all_position = spot[:, 0] * 64.0 + spot[:, 1]

    gathered = lax.all_gather(projected, "inst", axis=1, tiled=True)
    query = rotate(
        gathered[:, :width].astype(jnp.float32).reshape(n * rows, H, HD), all_position
    ).astype(jnp.bfloat16)
    query = query.reshape(n, rows, KVH, GROUPS, HD).transpose(0, 2, 1, 3, 4)
    query = query.reshape(n, KVH, rows * GROUPS, HD)

    slots = jnp.maximum(send_slots[0], 0)
    context = kv_pool[slots].reshape(n, cap * page_len, 2, KVH, HD)
    keys = context[:, :, 0]
    vals = context[:, :, 1]
    scores = (
        jnp.einsum("dkqf,dtkf->dkqt", query, keys, preferred_element_type=jnp.float32) * scale
    )
    within = jnp.arange(page_len)[None, None, :]
    valid = (within < (my_codes % 32)[:, :, None]).reshape(n, 1, cap * page_len)
    owner = jnp.broadcast_to((my_codes // 32)[:, :, None], (n, cap, page_len)).reshape(n, 1, -1)
    row_req = jnp.tile(jnp.repeat(jnp.arange(reqs), GROUPS), steps)[None, :, None]
    mask = (valid & (owner == row_req))[:, None]
    scores = jnp.where(mask, scores, MASKED)
    top = jnp.max(scores, axis=-1)
    weights = jnp.where(mask, jnp.exp(scores - top[..., None]), 0.0)
    total = jnp.sum(weights, axis=-1)
    mixed = jnp.einsum(
        "dkqt,dtkf->dkqf", weights.astype(jnp.bfloat16), vals, preferred_element_type=jnp.float32
    ).astype(jnp.bfloat16)
    stats = jnp.stack([top, total], axis=1)
    mixed = lax.all_to_all(mixed, "inst", split_axis=0, concat_axis=0, tiled=True)
    stats = lax.all_to_all(stats, "inst", split_axis=0, concat_axis=0, tiled=True)

    mine = lax.dynamic_slice_in_dim(gathered, me * rows, rows, axis=0)
    own_pos = position.astype(jnp.float32)
    own_query = lax.dynamic_index_in_dim(query, me, axis=0, keepdims=False)
    own_query = own_query.reshape(KVH, steps, reqs, GROUPS, HD)
    fresh_key = rotate(
        mine[:, width : width + half_width].astype(jnp.float32).reshape(rows, KVH, HD), own_pos
    ).astype(jnp.bfloat16)
    fresh_key = fresh_key.reshape(steps, reqs, KVH, HD)
    fresh_val = mine[:, width + half_width :].reshape(steps, reqs, KVH, HD)
    new_scores = (
        jnp.einsum("ksrgf,nrkf->ksrgn", own_query, fresh_key, preferred_element_type=jnp.float32)
        * scale
    )
    seen = jnp.arange(steps)[None, :] <= jnp.arange(steps)[:, None]
    seen = seen[None, :, None, None, :]
    new_scores = jnp.where(seen, new_scores, MASKED)
    tops = stats[:, 0].reshape(n, KVH, steps, reqs, GROUPS)
    totals = stats[:, 1].reshape(n, KVH, steps, reqs, GROUPS)
    best = jnp.maximum(jnp.max(tops, axis=0), jnp.max(new_scores, axis=-1))
    factors = jnp.exp(tops - best[None])
    new_weights = jnp.where(seen, jnp.exp(new_scores - best[..., None]), 0.0)
    total = jnp.sum(factors * totals, axis=0) + jnp.sum(new_weights, axis=-1)
    mixed = mixed.reshape(n, KVH, steps, reqs, GROUPS, HD).astype(jnp.float32)
    summed = jnp.sum(mixed * factors[..., None], axis=0)
    summed = summed + jnp.einsum(
        "ksrgn,nrkf->ksrgf",
        new_weights.astype(jnp.bfloat16),
        fresh_val,
        preferred_element_type=jnp.float32,
    )
    attended = (summed / total[..., None]).transpose(1, 2, 0, 3, 4)
    attended = attended.reshape(rows, width).astype(jnp.bfloat16)
    low_out = expand(attended, out_down, selector)
    both = jnp.concatenate([attended, jnp.pad(low_out, ((0, 0), (0, EXTRA - low)))], axis=1)
    every_att = lax.all_gather(both, "inst", axis=0, tiled=True)
    out_cols = columns(every_att[:, :width], every_att[:, width : width + low], out_weight, out_up)
    result = lax.all_to_all(out_cols, "inst", split_axis=0, concat_axis=1, tiled=True)
    return result.reshape(steps, reqs, width)


NZ, NY, NC = 4, 2, 2
NI = NZ * NY * NC
CHIPS = NZ * NY
ROWS = 4
ALL = NI * ROWS
BLK = 4
TOK = 512
KC = 4
FLOOR = -1e29


def send(src, dst, send_sem, recv_sem, to):
    copy = pltpu.make_async_remote_copy(
        src_ref=src,
        dst_ref=dst,
        send_sem=send_sem,
        recv_sem=recv_sem,
        device_id={"inst": to},
        device_id_type=pl.DeviceIdType.MESH,
    )
    copy.start()
    return copy


def index_of(z, y, c):
    return (z * NY + y) * NC + c


def gather_blocks(views, send_sems, recv_sems, me, use=None, between=None):
    z, y, c = me // (NY * NC), (me // NC) % NY, me % NC
    oy, oc = 1 - y, 1 - c
    started = []

    def put(block, to):
        slot = len(started)
        started.append([
            send(view(block), view(block), send_sems.at[v, slot], recv_sems.at[v, block], to)
            for v, view in enumerate(views)
        ])

    def arrive(block):
        for v, view in enumerate(views):
            pltpu.make_async_remote_copy(
                src_ref=view(block),
                dst_ref=view(block),
                send_sem=send_sems.at[v, 0],
                recv_sem=recv_sems.at[v, block],
                device_id={"inst": me},
                device_id_type=pl.DeviceIdType.MESH,
            ).wait_recv()

    for j in range(1, NZ):
        put(me, index_of((z + j) % NZ, y, c))
    put(me, index_of(z, oy, c))
    put(me, index_of(z, y, oc))
    if between is not None:
        between()
    if use is not None:
        use(me)
    for j in range(1, NZ):
        block = index_of((z + NZ - j) % NZ, y, c)
        arrive(block)
        put(block, index_of(z, oy, c))
        put(block, index_of(z, y, oc))
        if use is not None:
            use(block)
    for j in range(NZ):
        block = index_of((z + NZ - j) % NZ, oy, c)
        arrive(block)
        put(block, index_of(z, y, oc))
        if use is not None:
            use(block)
    for yy in (y, oy):
        for j in range(NZ):
            block = index_of((z + NZ - j) % NZ, yy, oc)
            arrive(block)
            if use is not None:
                use(block)
    for copies in started:
        for copy in copies:
            copy.wait_send()


def dot_t(a, b):
    return lax.dot_general(a, b, (((1,), (1,)), ((), ())), preferred_element_type=jnp.float32)


def block_kernel(
    slots_ref, x_ref, meta_ref, wq_ref, wo_ref, dq_ref, do_ref, uq_ref, uo_ref, pool_ref,
    out_ref,
    pool_v, ctx, wq_v, wo_v, x_all, meta_all, acc, proj, cc, ss, sel, nvr, heads,
    o_own, s_own, o_sib, s_sib, o_mrg, s_mrg, o_fin, s_fin, fbuf, att, oacc, fin, o_out, r_out,
    local_sem, g1s, g1r, g2s, g2r, sib_s, sib_r, fin_s, fin_r, g4s, g4r, os_sem, or_sem,
):
    me = lax.axis_index("inst")
    chip, core = me // NC, me % NC
    sibling = chip * NC + 1 - core
    scale = 1.0 / math.sqrt(HD)
    lowq, lowo = wq_ref.shape[0], wo_ref.shape[0]
    low = dq_ref.shape[0]

    loads = [
        pltpu.make_async_copy(pool_ref, pool_v, local_sem.at[0]),
        pltpu.make_async_copy(wq_ref, wq_v.at[pl.ds(0, lowq)], local_sem.at[1]),
        pltpu.make_async_copy(dq_ref, wq_v.at[pl.ds(lowq, low)], local_sem.at[2]),
        pltpu.make_async_copy(wo_ref, wo_v.at[pl.ds(0, lowo)], local_sem.at[3]),
        pltpu.make_async_copy(do_ref, wo_v.at[pl.ds(lowo, low)], local_sem.at[4]),
    ]
    for load in loads:
        load.start()

    barrier = pltpu.get_barrier_semaphore()
    for j in range(1, NI):
        pl.semaphore_signal(
            barrier, inc=1, device_id={"inst": (me + j) % NI},
            device_id_type=pl.DeviceIdType.MESH,
        )
    x_all[pl.ds(pl.multiple_of(me * 16, 16), 16), :] = x_ref[...]
    meta_all[me] = meta_ref[...]
    pl.semaphore_wait(barrier, NI - 1)

    def pages():
        loads[0].wait()

        def page(i, carry):
            slot = jnp.maximum(slots_ref[0, i], 0)
            ctx[pl.ds(pl.multiple_of(i * 16, 16), 16), :] = pool_v[slot]
            return carry

        lax.fori_loop(0, pool_ref.shape[0], page, 0)

    gather_blocks(
        [
            lambda i: x_all.at[pl.ds(pl.multiple_of(i * 16, 16), 16)],
            lambda i: meta_all.at[i],
        ],
        g1s, g1r, me, between=pages,
    )
    for d in range(NI):
        cc[pl.ds(4 * d, 4), :] = meta_all[d, 0:4, :]
        ss[pl.ds(4 * d, 4), :] = meta_all[d, 4:8, :]
        sel[pl.ds(4 * d, 4), :] = meta_all[d, 12:16, :]
        nvr[pl.ds(4 * d, 2), :] = meta_all[d, 8:10, :]
        nvr[pl.ds(4 * d + 2, 2), :] = meta_all[d, 8:10, :]
    lane = lax.broadcasted_iota(jnp.int32, (128, 128), 1)
    sub = lax.broadcasted_iota(jnp.int32, (128, 128), 0)
    pick = jnp.where(sub == me * 8 + lane // 16, 1.0, 0.0)
    nvx = jnp.dot(nvr[...], pick, preferred_element_type=jnp.float32)

    loads[1].wait()
    loads[2].wait()
    total_cols = lowq + low
    row_chunk = (lax.broadcasted_iota(jnp.int32, (NI * 16, 1), 0) // ROWS) % KC

    def chunk(kc, carry):
        at = pl.multiple_of(kc * 2048, 2048)
        for begin in range(0, total_cols, 256):
            size = min(256, total_cols - begin)
            part = dot_t(x_all[...], wq_v[pl.ds(begin, size), pl.ds(at, 2048)])
            old = acc[:, begin : begin + size]
            acc[:, begin : begin + size] = jnp.where(row_chunk == kc, part, old)
        return carry

    lax.fori_loop(0, KC, chunk, 0)
    for d in range(NI):
        piece = acc[16 * d : 16 * d + 8, :] + acc[16 * d + 8 : 16 * d + 16, :]
        proj[pl.ds(4 * d, 4), :] = piece[0:4] + piece[4:8]
    spread = (proj[:, lowq:] * sel[:, :low]).astype(jnp.bfloat16)
    extra = jnp.dot(spread, uq_ref[...], preferred_element_type=jnp.float32)
    own_heads = lowq // HD
    for i in range(own_heads):
        part = proj[:, i * HD : (i + 1) * HD] + extra[:, i * HD : (i + 1) * HD]
        part = part.astype(jnp.bfloat16).astype(jnp.float32)
        turned = part * cc[...] + pltpu.roll(part, HD // 2, 1) * ss[...]
        head = me * own_heads + i
        heads[head] = jnp.where(head < H + KVH, turned, part).astype(jnp.bfloat16)

    gather_blocks(
        [lambda i: heads.at[pl.ds(i * own_heads, own_heads)]], g2s, g2r, me,
    )

    row16 = lax.broadcasted_iota(jnp.int32, (16, 128), 0) // ROWS
    tok16 = (lax.broadcasted_iota(jnp.int32, (16, 128), 1) % 16).astype(jnp.float32)
    lane_of = lax.broadcasted_iota(jnp.int32, (128, 128), 1)

    def attend(k):
        stats = jnp.zeros((128, 128), jnp.float32)
        for b in range(BLK):
            limit = nvx[b * 16 : b * 16 + 16]
            open_ = jnp.where(tok16 < limit, 1.0, 0.0)
            mask = jnp.concatenate(
                [jnp.where(row16 == d, open_, 0.0) for d in range(4)], axis=1
            )
            mask = jnp.broadcast_to(mask[None], (GROUPS, 16, TOK)).reshape(128, TOK) > 0.5
            q = heads[pl.ds(k * GROUPS, GROUPS), b * 16 : b * 16 + 16, :].reshape(128, HD)
            keys = ctx[b * TOK : (b + 1) * TOK, pl.ds(pl.multiple_of(k * HD, HD), HD)]
            vals = ctx[
                b * TOK : (b + 1) * TOK, pl.ds(pl.multiple_of((KVH + k) * HD, HD), HD)
            ]
            s = jnp.where(mask, dot_t(q, keys) * scale, MASKED)
            top = jnp.maximum(jnp.max(s, axis=1, keepdims=True), FLOOR)
            p = jnp.exp(s - top)
            count = jnp.sum(p, axis=1, keepdims=True)
            o = jnp.dot(p.astype(jnp.bfloat16), vals, preferred_element_type=jnp.float32)
            o = o.astype(jnp.bfloat16).reshape(2, 4, 16, HD)
            o_own[k, :, :, b * 16 : b * 16 + 16, :] = o
            stats = jnp.where(lane_of == b, top, stats)
            stats = jnp.where(lane_of == BLK + b, count, stats)
        s_own[k] = stats.T[0:8]

    def to_sibling(k):
        return (
            pltpu.make_async_remote_copy(
                src_ref=o_own.at[k, 1 - core], dst_ref=o_sib.at[k],
                send_sem=sib_s.at[0, k], recv_sem=sib_r.at[0, k],
                device_id={"inst": sibling}, device_id_type=pl.DeviceIdType.MESH,
            ),
            pltpu.make_async_remote_copy(
                src_ref=s_own.at[k], dst_ref=s_sib.at[k],
                send_sem=sib_s.at[1, k], recv_sem=sib_r.at[1, k],
                device_id={"inst": sibling}, device_id_type=pl.DeviceIdType.MESH,
            ),
        )

    def to_owner(k):
        return (
            pltpu.make_async_remote_copy(
                src_ref=o_mrg.at[k], dst_ref=o_fin.at[chip],
                send_sem=fin_s.at[0, k], recv_sem=fin_r.at[0, chip],
                device_id={"inst": k * NC + core}, device_id_type=pl.DeviceIdType.MESH,
            ),
            pltpu.make_async_remote_copy(
                src_ref=s_mrg.at[k], dst_ref=s_fin.at[chip],
                send_sem=fin_s.at[1, k], recv_sem=fin_r.at[1, chip],
                device_id={"inst": k * NC + core}, device_id_type=pl.DeviceIdType.MESH,
            ),
        )

    def factors(rows):
        pad = jnp.zeros((128 - rows.shape[0], 128), jnp.float32)
        fbuf[...] = jnp.concatenate([rows, pad], axis=0).T
        return fbuf[pl.ds(pl.multiple_of(core * 64, 64), 64), :]

    def merge(k):
        for copy in to_sibling(k):
            copy.wait_recv()
        s1, s2 = s_own[k], s_sib[k]
        top = jnp.maximum(s1[0:4], s2[0:4])
        f1, f2 = jnp.exp(s1[0:4] - top), jnp.exp(s2[0:4] - top)
        s_mrg[k] = jnp.concatenate([top, s1[4:8] * f1 + s2[4:8] * f2], axis=0)
        f = factors(jnp.concatenate([f1, f2], axis=0))
        for b in range(BLK):
            o1 = o_own[k, core, :, b * 16 : b * 16 + 16, :].reshape(64, HD).astype(jnp.float32)
            o2 = o_sib[k, :, b * 16 : b * 16 + 16, :].reshape(64, HD).astype(jnp.float32)
            o = o1 * f[:, b : b + 1] + o2 * f[:, 4 + b : 5 + b]
            o_mrg[k, :, b * 16 : b * 16 + 16, :] = o.astype(jnp.bfloat16).reshape(4, 16, HD)

    def merge_and_send(j):
        k = (chip + 1 + j) % CHIPS
        merge(k)
        for copy in to_owner(k):
            copy.start()

    def step(j, carry):
        k = (chip + 1 + j) % CHIPS
        attend(k)
        for copy in to_sibling(k):
            copy.start()

        @pl.when(j > 0)
        def _():
            merge_and_send(j - 1)

        return carry

    lax.fori_loop(0, CHIPS, step, 0)
    merge(chip)
    o_fin[chip] = o_mrg[chip]
    s_fin[chip] = s_mrg[chip]

    key = heads[H + chip].astype(jnp.float32)
    val = heads[H + KVH + chip].astype(jnp.float32)
    old_key, old_val = pltpu.roll(key, 2, 0), pltpu.roll(val, 2, 0)
    is_later = (lax.broadcasted_iota(jnp.int32, (64, 1), 0) % ROWS) >= 2
    stats = jnp.zeros((64, 128), jnp.float32)
    lane64 = lax.broadcasted_iota(jnp.int32, (64, 128), 1)
    fresh = []
    for b in range(BLK):
        def wide(a):
            a = a[b * 16 : b * 16 + 16]
            return jnp.broadcast_to(a[None], (4, 16, HD)).reshape(64, HD)

        q = heads[pl.ds(me * 4, 4), b * 16 : b * 16 + 16, :].reshape(64, HD).astype(jnp.float32)
        own = jnp.sum(q * wide(key), axis=1, keepdims=True) * scale
        prev = jnp.sum(q * wide(old_key), axis=1, keepdims=True) * scale
        prev = jnp.where(is_later, prev, MASKED)
        top = jnp.maximum(own, prev)
        w0, w1 = jnp.exp(own - top), jnp.exp(prev - top)
        stats = jnp.where(lane64 == b, top, stats)
        stats = jnp.where(lane64 == BLK + b, w0 + w1, stats)
        w0 = w0.astype(jnp.bfloat16).astype(jnp.float32)
        w1 = w1.astype(jnp.bfloat16).astype(jnp.float32)
        fresh.append(w0 * wide(val) + w1 * wide(old_val))
    s_new = jnp.concatenate([stats, stats], axis=0).T[0:8]

    def wait_owner(j, carry):
        source = (chip + CHIPS - 1 - j) % CHIPS
        for copy in (
            pltpu.make_async_remote_copy(
                src_ref=o_mrg.at[source], dst_ref=o_fin.at[source],
                send_sem=fin_s.at[0, source], recv_sem=fin_r.at[0, source],
                device_id={"inst": sibling}, device_id_type=pl.DeviceIdType.MESH,
            ),
            pltpu.make_async_remote_copy(
                src_ref=s_mrg.at[source], dst_ref=s_fin.at[source],
                send_sem=fin_s.at[1, source], recv_sem=fin_r.at[1, source],
                device_id={"inst": sibling}, device_id_type=pl.DeviceIdType.MESH,
            ),
        ):
            copy.wait_recv()
        return carry

    lax.fori_loop(0, CHIPS - 1, wait_owner, 0)
    every = [s_fin[i] for i in range(CHIPS)] + [s_new]
    top = functools.reduce(jnp.maximum, [s[0:4] for s in every])
    shares = [jnp.exp(s[0:4] - top) for s in every]
    total = sum(s[4:8] * f for s, f in zip(every, shares))
    f = factors(jnp.concatenate([f / total for f in shares], axis=0))
    for b in range(BLK):
        o = fresh[b] * f[:, CHIPS * 4 + b : CHIPS * 4 + b + 1]
        for i in range(CHIPS):
            part = o_fin[i, :, b * 16 : b * 16 + 16, :].reshape(64, HD).astype(jnp.float32)
            o = o + part * f[:, i * 4 + b : i * 4 + b + 1]
        o = o.astype(jnp.bfloat16)
        for g in range(4):
            att[me, b * 16 : b * 16 + 16, g * HD : (g + 1) * HD] = o[g * 16 : g * 16 + 16]

    loads[3].wait()
    loads[4].wait()
    oacc[...] = jnp.zeros_like(oacc)

    def use(i):
        at = pl.multiple_of(i * 512, 512)
        oacc[...] += dot_t(att[i], wo_v[:, pl.ds(at, 512)])

    gather_blocks([lambda i: att.at[i]], g4s, g4r, me, use=use)
    spread = (oacc[:, lowo:] * sel[:, :low]).astype(jnp.bfloat16)
    fin[...] = oacc[:, :lowo] + jnp.dot(spread, uo_ref[...], preferred_element_type=jnp.float32)
    for d in range(NI):
        piece = jnp.concatenate(
            [fin[pl.ds(4 * d, 4), i * 128 : (i + 1) * 128] for i in range(4)], axis=0
        )
        o_out[d] = piece.astype(jnp.bfloat16)
    r_out[me] = o_out[me]
    outs = []
    for j in range(1, NI):
        to = (me + j) % NI
        outs.append(send(o_out.at[to], r_out.at[me], os_sem.at[j], or_sem.at[j], to))
    for copy in outs:
        copy.wait_recv()
    out_ref[...] = r_out[...]

    def sent(j, carry):
        for copy in to_sibling(j):
            copy.wait_send()

        @pl.when(j != chip)
        def _():
            for copy in to_owner(j):
                copy.wait_send()

        return carry

    lax.fori_loop(0, CHIPS, sent, 0)
    for copy in outs:
        copy.wait_send()


def one_kernel(slots, x, meta, wq, wo, dq, do, uq, uo, pool):
    vm = pl.BlockSpec(memory_space=pltpu.VMEM)
    hbm = pl.BlockSpec(memory_space=pl.ANY)
    bf, f32 = jnp.bfloat16, jnp.float32
    qcols, ocols, low, width = wq.shape[0], wo.shape[0], dq.shape[0], wq.shape[1]
    V = pltpu.VMEM
    dma = pltpu.SemaphoreType.DMA
    return pl.pallas_call(
        block_kernel,
        out_shape=jax.ShapeDtypeStruct((NI, 16, 128), bf),
        in_specs=[pl.BlockSpec(memory_space=pltpu.SMEM), vm, vm, hbm, hbm, hbm, hbm, vm, vm, hbm],
        out_specs=vm,
        scratch_shapes=[
            V(pool.shape, bf),
            V((pool.shape[0] * 16, pool.shape[2]), bf),
            V((qcols + low, width), bf),
            V((ocols + low, width), bf),
            V((NI * 16, 2048), bf),
            V((NI, 16, 128), f32),
            V((NI * 16, qcols + low), f32),
            V((ALL, qcols + low), f32),
            V((ALL, 128), f32),
            V((ALL, 128), f32),
            V((ALL, 128), f32),
            V((ALL, 128), f32),
            V((H + 2 * KVH, ALL, HD), bf),
            V((KVH, 2, 4, ALL, HD), bf),
            V((KVH, 8, 128), f32),
            V((KVH, 4, ALL, HD), bf),
            V((KVH, 8, 128), f32),
            V((KVH, 4, ALL, HD), bf),
            V((KVH, 8, 128), f32),
            V((KVH, 4, ALL, HD), bf),
            V((KVH, 8, 128), f32),
            V((128, 128), f32),
            V((NI, ALL, 512), bf),
            V((ALL, ocols + low), f32),
            V((ALL, ocols), f32),
            V((NI, 16, 128), bf),
            V((NI, 16, 128), bf),
            dma((5,)),
            dma((2, NI)), dma((2, NI)),
            dma((1, NI)), dma((1, NI)),
            dma((2, KVH)), dma((2, KVH)),
            dma((2, KVH)), dma((2, KVH)),
            dma((1, NI)), dma((1, NI)),
            dma((NI,)), dma((NI,)),
        ],
        compiler_params=pltpu.CompilerParams(
            collective_id=0, has_side_effects=True, vmem_limit_bytes=58 * 1024 * 1024
        ),
        name="attention_block",
    )(slots, x, meta, wq, wo, dq, do, uq, uo, pool)


def per_device_16(
    tokens, norm_gain, qkv_weight, out_weight, qkv_down, qkv_up, out_down, out_up,
    adapter_ids, cached_len, page_table, send_slots, kv_pool,
):
    steps, reqs, width = tokens.shape
    adapters, rank = qkv_down.shape[:2]
    low = adapters * rank
    rows = steps * reqs
    page_len = kv_pool.shape[1]
    normed = normalize(tokens, norm_gain).reshape(rows, KC, width // KC)
    x = normed.transpose(1, 0, 2).reshape(rows * KC, width // KC)
    position = jnp.concatenate([cached_len + s for s in range(steps)]).astype(jnp.float32)
    half = HD // 2
    freqs = ROPE_BASE ** (-(jnp.arange(half, dtype=jnp.float32) * 2.0) / HD)
    angle = position[:, None] * freqs
    cosine, sine = jnp.cos(angle), jnp.sin(angle)
    begins = jnp.arange(page_table.shape[1], dtype=jnp.int32) * page_len
    valid = jnp.clip(cached_len[:, None] - begins[None, :], 0, page_len)
    arrivals = jnp.arange(send_slots.shape[1], dtype=jnp.int32)
    match = page_table[:, :, None] == arrivals[None, None, :]
    counts = jnp.sum(jnp.where(match, valid[:, :, None], 0), axis=1).astype(jnp.float32)
    chosen = adapter_ids[:, None] == (jnp.arange(128) // rank)[None, :]
    selector = jnp.tile(chosen.astype(jnp.float32), (steps, 1))
    meta = jnp.concatenate(
        [
            jnp.concatenate([cosine, cosine], axis=1),
            jnp.concatenate([-sine, sine], axis=1),
            counts,
            jnp.zeros((2, 128), jnp.float32),
            selector,
        ],
        axis=0,
    )
    out = one_kernel(
        send_slots, x, meta, qkv_weight, out_weight,
        qkv_down.reshape(low, width), out_down.reshape(low, width),
        qkv_up.reshape(low, -1), out_up.reshape(low, -1), kv_pool,
    )
    out = out.reshape(NI, 4, rows, 128).transpose(2, 0, 1, 3)
    return out.reshape(steps, reqs, width)


def solution(mesh):
    in_specs = (
        P(None, ("dom", "inst"), None),
        P(),
        P("inst", None),
        P("inst", None),
        P(),
        P(None, None, "inst"),
        P(),
        P(None, None, "inst"),
        P(("dom", "inst")),
        P(("dom", "inst")),
        P(("dom", "inst"), None),
        P(("dom", "inst"), None),
        P(("dom", "inst"), None, None),
    )
    out_specs = P(None, ("dom", "inst"), None)
    n = mesh.shape["inst"]
    return jax.shard_map(
        per_device_16 if n == NI else functools.partial(per_device, n),
        mesh=mesh,
        in_specs=in_specs,
        out_specs=out_specs,
        check_vma=False,
    )
```

```python
import functools
import math

import jax
import jax.numpy as jnp
import numpy as np
from jax import lax
from jax.experimental import pallas as pl
from jax.experimental.pallas import tpu as pltpu
from jax.sharding import PartitionSpec as P

H = 64
KVH = 8
HD = 128
GROUPS = H // KVH
EXTRA = 128

EPSILON = 1e-05
ROPE_BASE = 500000.0
MASKED = -1e30


def rotate(vectors, position):
    half = vectors.shape[-1] // 2
    freqs = ROPE_BASE ** (-(jnp.arange(half, dtype=jnp.float32) * 2.0) / vectors.shape[-1])
    angle = position[:, None, None] * freqs
    cosine = jnp.cos(angle)
    sine = jnp.sin(angle)
    first = vectors[..., :half]
    second = vectors[..., half:]
    return jnp.concatenate(
        [first * cosine - second * sine, second * cosine + first * sine], axis=-1
    )


def normalize(hidden, norm_gain):
    values = hidden.astype(jnp.float32)
    factor = lax.rsqrt(jnp.mean(values * values, axis=-1, keepdims=True) + EPSILON)
    return (values * factor * norm_gain.astype(jnp.float32)).astype(jnp.bfloat16)


def expand(rows, down_maps, selector):
    every = jnp.einsum("rd,akd->rak", rows, down_maps, preferred_element_type=jnp.float32)
    chosen = jnp.sum(every * selector[:, :, None], axis=1).astype(jnp.bfloat16)
    spread = selector[:, :, None] * chosen[:, None, :].astype(jnp.float32)
    return spread.reshape(rows.shape[0], -1).astype(jnp.bfloat16)


def columns(gathered, spread, weight, up_maps):
    base = lax.dot_general(
        gathered, weight, (((1,), (1,)), ((), ())), preferred_element_type=jnp.float32
    )
    extra = jnp.dot(
        spread, up_maps.reshape(-1, up_maps.shape[2]), preferred_element_type=jnp.float32
    )
    return (base + extra).astype(jnp.bfloat16)


def page_codes(page_table, cached_len, page_len):
    reqs, maxp = page_table.shape
    begins = jnp.arange(maxp, dtype=jnp.int32) * page_len
    valid = jnp.clip(cached_len[:, None] - begins[None, :], 0, page_len)
    code = valid + 32 * jnp.arange(reqs, dtype=jnp.int32)[:, None]
    rows = jnp.arange(reqs * maxp, dtype=jnp.int32)
    match = page_table.reshape(-1)[:, None] == rows[None, :]
    return jnp.sum(jnp.where(match, code.reshape(-1)[:, None], 0), axis=0)


def per_device(
    n,
    tokens,
    norm_gain,
    qkv_weight,
    out_weight,
    qkv_down,
    qkv_up,
    out_down,
    out_up,
    adapter_ids,
    cached_len,
    page_table,
    send_slots,
    kv_pool,
):
    steps, reqs, width = tokens.shape
    adapters, rank = qkv_down.shape[:2]
    half_width = KVH * HD
    page_len = kv_pool.shape[1]
    pages = send_slots.shape[1]
    cap = pages // n
    rows = steps * reqs
    scale = 1.0 / math.sqrt(HD)
    me = lax.axis_index("inst")

    selector = (adapter_ids[:, None] == jnp.arange(adapters)[None, :]).astype(jnp.float32)
    selector = jnp.tile(selector, (steps, 1))
    normed = normalize(tokens, norm_gain).reshape(rows, width)
    spread = expand(normed, qkv_down, selector)
    codes = page_codes(page_table, cached_len, page_len)
    position = jnp.concatenate([cached_len + s for s in range(steps)])
    extra = jnp.concatenate(
        [
            spread,
            codes.reshape(rows, -1).astype(jnp.bfloat16),
            (position // 64).astype(jnp.bfloat16)[:, None],
            (position % 64).astype(jnp.bfloat16)[:, None],
        ],
        axis=1,
    )
    extra = jnp.pad(extra, ((0, 0), (0, EXTRA - extra.shape[1])))
    sent = jnp.concatenate([normed, extra], axis=1)
    everyone = lax.all_gather(sent, "inst", axis=0, tiled=True)
    low = adapters * rank
    per_row = pages // rows
    projected = columns(everyone[:, :width], everyone[:, width : width + low], qkv_weight, qkv_up)
    all_codes = everyone[:, width + low : width + low + per_row].astype(jnp.int32)
    my_codes = lax.dynamic_slice_in_dim(all_codes.reshape(n, pages), me * cap, cap, axis=1)
    spot = everyone[:, width + low + per_row : width + low + per_row + 2].astype(jnp.float32)
    all_position = spot[:, 0] * 64.0 + spot[:, 1]

    gathered = lax.all_gather(projected, "inst", axis=1, tiled=True)
    query = rotate(
        gathered[:, :width].astype(jnp.float32).reshape(n * rows, H, HD), all_position
    ).astype(jnp.bfloat16)
    query = query.reshape(n, rows, KVH, GROUPS, HD).transpose(0, 2, 1, 3, 4)
    query = query.reshape(n, KVH, rows * GROUPS, HD)

    slots = jnp.maximum(send_slots[0], 0)
    context = kv_pool[slots].reshape(n, cap * page_len, 2, KVH, HD)
    keys = context[:, :, 0]
    vals = context[:, :, 1]
    scores = (
        jnp.einsum("dkqf,dtkf->dkqt", query, keys, preferred_element_type=jnp.float32) * scale
    )
    within = jnp.arange(page_len)[None, None, :]
    valid = (within < (my_codes % 32)[:, :, None]).reshape(n, 1, cap * page_len)
    owner = jnp.broadcast_to((my_codes // 32)[:, :, None], (n, cap, page_len)).reshape(n, 1, -1)
    row_req = jnp.tile(jnp.repeat(jnp.arange(reqs), GROUPS), steps)[None, :, None]
    mask = (valid & (owner == row_req))[:, None]
    scores = jnp.where(mask, scores, MASKED)
    top = jnp.max(scores, axis=-1)
    weights = jnp.where(mask, jnp.exp(scores - top[..., None]), 0.0)
    total = jnp.sum(weights, axis=-1)
    mixed = jnp.einsum(
        "dkqt,dtkf->dkqf", weights.astype(jnp.bfloat16), vals, preferred_element_type=jnp.float32
    ).astype(jnp.bfloat16)
    stats = jnp.stack([top, total], axis=1)
    mixed = lax.all_to_all(mixed, "inst", split_axis=0, concat_axis=0, tiled=True)
    stats = lax.all_to_all(stats, "inst", split_axis=0, concat_axis=0, tiled=True)

    mine = lax.dynamic_slice_in_dim(gathered, me * rows, rows, axis=0)
    own_pos = position.astype(jnp.float32)
    own_query = lax.dynamic_index_in_dim(query, me, axis=0, keepdims=False)
    own_query = own_query.reshape(KVH, steps, reqs, GROUPS, HD)
    fresh_key = rotate(
        mine[:, width : width + half_width].astype(jnp.float32).reshape(rows, KVH, HD), own_pos
    ).astype(jnp.bfloat16)
    fresh_key = fresh_key.reshape(steps, reqs, KVH, HD)
    fresh_val = mine[:, width + half_width :].reshape(steps, reqs, KVH, HD)
    new_scores = (
        jnp.einsum("ksrgf,nrkf->ksrgn", own_query, fresh_key, preferred_element_type=jnp.float32)
        * scale
    )
    seen = jnp.arange(steps)[None, :] <= jnp.arange(steps)[:, None]
    seen = seen[None, :, None, None, :]
    new_scores = jnp.where(seen, new_scores, MASKED)
    tops = stats[:, 0].reshape(n, KVH, steps, reqs, GROUPS)
    totals = stats[:, 1].reshape(n, KVH, steps, reqs, GROUPS)
    best = jnp.maximum(jnp.max(tops, axis=0), jnp.max(new_scores, axis=-1))
    factors = jnp.exp(tops - best[None])
    new_weights = jnp.where(seen, jnp.exp(new_scores - best[..., None]), 0.0)
    total = jnp.sum(factors * totals, axis=0) + jnp.sum(new_weights, axis=-1)
    mixed = mixed.reshape(n, KVH, steps, reqs, GROUPS, HD).astype(jnp.float32)
    summed = jnp.sum(mixed * factors[..., None], axis=0)
    summed = summed + jnp.einsum(
        "ksrgn,nrkf->ksrgf",
        new_weights.astype(jnp.bfloat16),
        fresh_val,
        preferred_element_type=jnp.float32,
    )
    attended = (summed / total[..., None]).transpose(1, 2, 0, 3, 4)
    attended = attended.reshape(rows, width).astype(jnp.bfloat16)
    low_out = expand(attended, out_down, selector)
    both = jnp.concatenate([attended, jnp.pad(low_out, ((0, 0), (0, EXTRA - low)))], axis=1)
    every_att = lax.all_gather(both, "inst", axis=0, tiled=True)
    out_cols = columns(every_att[:, :width], every_att[:, width : width + low], out_weight, out_up)
    result = lax.all_to_all(out_cols, "inst", split_axis=0, concat_axis=1, tiled=True)
    return result.reshape(steps, reqs, width)


NZ, NY, NC = 4, 2, 2
NI = NZ * NY * NC
CHIPS = NZ * NY
ROWS = 4
ALL = NI * ROWS
BLK = 4
TOK = 512
KC = 4
FLOOR = -1e29


def send(src, dst, send_sem, recv_sem, to):
    copy = pltpu.make_async_remote_copy(
        src_ref=src,
        dst_ref=dst,
        send_sem=send_sem,
        recv_sem=recv_sem,
        device_id={"inst": to},
        device_id_type=pl.DeviceIdType.MESH,
    )
    copy.start()
    return copy


def index_of(z, y, c):
    return (z * NY + y) * NC + c


class Gather:
    def __init__(self, pieces, send_sems, recv_sems, me):
        self.pieces, self.send_sems, self.recv_sems, self.me = pieces, send_sems, recv_sems, me
        self.z, self.y, self.c = me // (NY * NC), (me // NC) % NY, me % NC
        self.first = [sum(len(q) for q in pieces[:p]) for p in range(len(pieces))]
        self.slots = [0] * len(pieces)
        self.started = []

    def put(self, p, block, to):
        slot = self.slots[p]
        self.slots[p] += 1
        for v, view in enumerate(self.pieces[p], self.first[p]):
            self.started.append(
                send(view(block), view(block), self.send_sems.at[v, slot],
                     self.recv_sems.at[v, block], to)
            )

    def arrive(self, p, block):
        for v, view in enumerate(self.pieces[p], self.first[p]):
            pltpu.make_async_remote_copy(
                src_ref=view(block),
                dst_ref=view(block),
                send_sem=self.send_sems.at[v, 0],
                recv_sem=self.recv_sems.at[v, block],
                device_id={"inst": self.me},
                device_id_type=pl.DeviceIdType.MESH,
            ).wait_recv()

    def issue(self, p):
        z, y, c = self.z, self.y, self.c
        for j in range(1, NZ):
            self.put(p, self.me, index_of((z + j) % NZ, y, c))
        self.put(p, self.me, index_of(z, 1 - y, c))
        self.put(p, self.me, index_of(z, y, 1 - c))

    def drain(self, use=None, fillers=()):
        z, y, c = self.z, self.y, self.c
        fillers = list(fillers)
        pending = []

        def idle():
            if pending:
                use(*pending.pop(0))
            elif fillers:
                fillers.pop(0)()

        def done(p, block):
            if use is not None:
                pending.append((block, p))
            idle()

        def from_z(p):
            for j in range(1, NZ):
                block = index_of((z + NZ - j) % NZ, y, c)
                self.arrive(p, block)
                self.put(p, block, index_of(z, 1 - y, c))
                self.put(p, block, index_of(z, y, 1 - c))
                done(p, block)

        def from_y(p):
            for j in range(NZ):
                block = index_of((z + NZ - j) % NZ, 1 - y, c)
                self.arrive(p, block)
                self.put(p, block, index_of(z, y, 1 - c))
                done(p, block)

        count = len(self.pieces)
        if use is not None:
            pending.extend((self.me, p) for p in range(count))
        idle()
        for p in range(count):
            from_z(p)
            if p > 0:
                from_y(p - 1)
        from_y(count - 1)
        for p in range(count):
            for yy in (y, 1 - y):
                for j in range(NZ):
                    block = index_of((z + NZ - j) % NZ, yy, 1 - c)
                    self.arrive(p, block)
                    done(p, block)
        while pending or fillers:
            idle()

    def finish(self):
        for copy in self.started:
            copy.wait_send()


def dot_t(a, b):
    return lax.dot_general(a, b, (((1,), (1,)), ((), ())), preferred_element_type=jnp.float32)


def block_kernel(
    slots_ref, len_ref, adapter_ref, tok_ref, gain_ref, freq_ref, table_ref, wq_ref, wo_ref, dq_ref, do_ref, uq_ref, uo_ref, pool_ref,
    out_ref,
    pool_v, ctx, wq_v, wo_v, x_f, x_all, meta_all, acc, proj, cc, ss, sel, nvr, bias, heads,
    o_own, s_own, o_sib, s_sib, o_mrg, s_mrg, o_fin, s_fin, fbuf, att, oacc, fin, o_out, r_out,
    local_sem, g1s, g1r, g2s, g2r, sib_s, sib_r, fin_s, fin_r, g4s, g4r, os_sem, or_sem,
):
    me = lax.axis_index("inst")
    chip, core = me // NC, me % NC
    sibling = chip * NC + 1 - core
    scale2 = math.log2(math.e) / math.sqrt(HD)
    lowq, lowo = wq_ref.shape[0], wo_ref.shape[0]
    low = dq_ref.shape[0]

    loads = [
        pltpu.make_async_copy(pool_ref, pool_v, local_sem.at[0]),
        pltpu.make_async_copy(wq_ref, wq_v.at[pl.ds(0, lowq)], local_sem.at[1]),
        pltpu.make_async_copy(dq_ref, wq_v.at[pl.ds(lowq, low)], local_sem.at[2]),
        pltpu.make_async_copy(wo_ref, wo_v.at[pl.ds(0, lowo)], local_sem.at[3]),
        pltpu.make_async_copy(do_ref, wo_v.at[pl.ds(lowo, low)], local_sem.at[4]),
    ]
    for load in loads:
        load.start()

    barrier = pltpu.get_barrier_semaphore()
    for j in range(1, NI):
        pl.semaphore_signal(
            barrier, inc=1, device_id={"inst": (me + j) % NI},
            device_id_type=pl.DeviceIdType.MESH,
        )
    gain = gain_ref[...].astype(jnp.float32)
    for s in range(2):
        values = tok_ref[s].astype(jnp.float32)
        mean = jnp.sum(values * values, axis=-1, keepdims=True) / values.shape[-1]
        values = values * lax.rsqrt(mean + EPSILON) * gain
        for kc in range(KC):
            x_f[pl.ds(kc * 4 + 2 * s, 2), :] = values[:, kc * 2048 : (kc + 1) * 2048]
    x_all[pl.ds(pl.multiple_of(me * 16, 16), 16), :] = x_f[...].astype(jnp.bfloat16)
    lane = lax.broadcasted_iota(jnp.int32, (128, 128), 1)
    sub = lax.broadcasted_iota(jnp.int32, (128, 128), 0)
    row8 = lax.broadcasted_iota(jnp.int32, (8, 128), 0)
    lane8 = lax.broadcasted_iota(jnp.int32, (8, 128), 1)
    req8 = row8 % 2
    length = jnp.where(req8 == 0, len_ref[0], len_ref[1])
    position = (length + (row8 // 2) % 2).astype(jnp.float32)
    angle = position * freq_ref[...]
    sine = jnp.sin(angle)
    sine = jnp.where(lane8 < HD // 2, -sine, sine)
    meta_all[me, pl.ds(0, 8), :] = jnp.where(row8 < 4, jnp.cos(angle), sine)
    counts = jnp.zeros((128, 128), jnp.float32)
    maxp = table_ref.shape[1]
    begin = lax.broadcasted_iota(jnp.int32, (1, maxp), 1) * 16
    for r in range(2):
        valid = jnp.clip(len_ref[r] - begin, 0, 16).astype(jnp.float32)
        hit = jnp.broadcast_to(table_ref[r : r + 1, :], (128, maxp)) == sub[:, :maxp]
        column = jnp.sum(jnp.where(hit, valid, 0.0), axis=1, keepdims=True)
        counts = jnp.where(lane == r, column, counts)
    adapter = jnp.where(req8 == 0, adapter_ref[0], adapter_ref[1])
    chosen = jnp.where(lane8 // 16 == adapter, 1.0, 0.0)
    meta_all[me, pl.ds(8, 8), :] = jnp.where(row8 < 4, counts.T[0:8], chosen)
    pl.semaphore_wait(barrier, NI - 1)

    def x_view(p):
        return lambda i: x_all.at[
            pl.ds(pl.multiple_of(i * 16, 16), 16), pl.ds(p * 1024, 1024)
        ]

    first = Gather([[x_view(0)], [x_view(1), lambda i: meta_all.at[i]]], g1s, g1r, me)
    for p in range(2):
        first.issue(p)
    first.drain()
    for d in range(NI):
        cc[pl.ds(4 * d, 4), :] = meta_all[d, 0:4, :]
        ss[pl.ds(4 * d, 4), :] = meta_all[d, 4:8, :]
        sel[pl.ds(4 * d, 4), :] = meta_all[d, 12:16, :]
        nvr[pl.ds(4 * d, 2), :] = meta_all[d, 8:10, :]
        nvr[pl.ds(4 * d + 2, 2), :] = meta_all[d, 8:10, :]
    pick = jnp.where(sub == me * 8 + lane // 16, 1.0, 0.0)
    nvx = jnp.dot(nvr[...], pick, preferred_element_type=jnp.float32)

    row16 = lax.broadcasted_iota(jnp.int32, (16, 128), 0) // ROWS
    tok16 = (lax.broadcasted_iota(jnp.int32, (16, 128), 1) % 16).astype(jnp.float32)
    for b in range(BLK):
        shown = jnp.where(tok16 < nvx[b * 16 : b * 16 + 16], 0.0, MASKED)
        for d in range(4):
            bias[b, :, d * 128 : (d + 1) * 128] = jnp.where(row16 == d, shown, MASKED)

    loads[1].wait()
    loads[2].wait()
    row_chunk = (lax.broadcasted_iota(jnp.int32, (NI * 16, 1), 0) // ROWS) % KC
    own_heads = lowq // HD
    tiles = [(4, 1), (0, 2), (2, 2)]
    second = Gather(
        [
            [lambda i, at=at, n=n: heads.at[pl.ds(i * own_heads + at, n)]]
            for at, n in tiles
        ],
        g2s, g2r, me,
    )
    spread = None
    for p, (head_at, count) in enumerate(tiles):
        begin = head_at * HD
        size = count * HD + (low if p == 0 else 0)

        def chunk(kc, carry, begin=begin, size=size):
            at = pl.multiple_of(kc * 2048, 2048)
            part = dot_t(x_all[...], wq_v[pl.ds(begin, size), pl.ds(at, 2048)])
            acc[:, :size] = jnp.where(row_chunk == kc, part, acc[:, :size])
            return carry

        lax.fori_loop(0, KC, chunk, 0)
        for d in range(NI):
            piece = acc[16 * d : 16 * d + 8, :size] + acc[16 * d + 8 : 16 * d + 16, :size]
            proj[pl.ds(4 * d, 4), :size] = piece[0:4] + piece[4:8]
        if p == 0:
            spread = (proj[:, HD : HD + low] * sel[:, :low]).astype(jnp.bfloat16)
        extra = jnp.dot(
            spread, uq_ref[:, begin : begin + count * HD], preferred_element_type=jnp.float32
        )
        for i in range(count):
            part = proj[:, i * HD : (i + 1) * HD] + extra[:, i * HD : (i + 1) * HD]
            part = part.astype(jnp.bfloat16).astype(jnp.float32)
            turned = part * cc[...] + pltpu.roll(part, HD // 2, 1) * ss[...]
            head = me * own_heads + head_at + i
            heads[head] = jnp.where(head < H + KVH, turned, part).astype(jnp.bfloat16)
        second.issue(p)

    loads[0].wait()

    def page(i, carry):
        slot = jnp.maximum(slots_ref[0, i], 0)
        ctx[pl.ds(pl.multiple_of(i * 16, 16), 16), :] = pool_v[slot]
        return carry

    pages = pool_ref.shape[0]
    second.drain(
        fillers=[
            lambda q=q: lax.fori_loop(q * pages // 8, (q + 1) * pages // 8, page, 0)
            for q in range(8)
        ]
    )

    def attend(k):
        stats = jnp.zeros((128, 128), jnp.float32)
        for b in range(BLK):
            q = heads[pl.ds(k * GROUPS, GROUPS), b * 16 : b * 16 + 16, :].reshape(128, HD)
            keys = ctx[b * TOK : (b + 1) * TOK, pl.ds(pl.multiple_of(k * HD, HD), HD)]
            vals = ctx[
                b * TOK : (b + 1) * TOK, pl.ds(pl.multiple_of((KVH + k) * HD, HD), HD)
            ]
            s = dot_t(q, keys).reshape(GROUPS, 16, TOK) + bias[b][None]
            s = s.reshape(128, TOK)
            top = jnp.maximum(jnp.max(s, axis=1, keepdims=True), FLOOR)
            p = jnp.exp2((s - top) * scale2)
            count = jnp.sum(p, axis=1, keepdims=True)
            o = jnp.dot(p.astype(jnp.bfloat16), vals, preferred_element_type=jnp.float32)
            o = o.astype(jnp.bfloat16).reshape(2, 4, 16, HD)
            o_own[k, :, :, b * 16 : b * 16 + 16, :] = o
            stats = jnp.where(lane == b, top, stats)
            stats = jnp.where(lane == BLK + b, count, stats)
        s_own[k] = stats.T[0:8]

    def to_sibling(k):
        return (
            pltpu.make_async_remote_copy(
                src_ref=o_own.at[k, 1 - core], dst_ref=o_sib.at[k],
                send_sem=sib_s.at[0, k], recv_sem=sib_r.at[0, k],
                device_id={"inst": sibling}, device_id_type=pl.DeviceIdType.MESH,
            ),
            pltpu.make_async_remote_copy(
                src_ref=s_own.at[k], dst_ref=s_sib.at[k],
                send_sem=sib_s.at[1, k], recv_sem=sib_r.at[1, k],
                device_id={"inst": sibling}, device_id_type=pl.DeviceIdType.MESH,
            ),
        )

    def to_owner(k):
        return (
            pltpu.make_async_remote_copy(
                src_ref=o_mrg.at[k], dst_ref=o_fin.at[chip],
                send_sem=fin_s.at[0, k], recv_sem=fin_r.at[0, chip],
                device_id={"inst": k * NC + core}, device_id_type=pl.DeviceIdType.MESH,
            ),
            pltpu.make_async_remote_copy(
                src_ref=s_mrg.at[k], dst_ref=s_fin.at[chip],
                send_sem=fin_s.at[1, k], recv_sem=fin_r.at[1, chip],
                device_id={"inst": k * NC + core}, device_id_type=pl.DeviceIdType.MESH,
            ),
        )

    def factors(rows):
        pad = jnp.zeros((128 - rows.shape[0], 128), jnp.float32)
        fbuf[...] = jnp.concatenate([rows, pad], axis=0).T
        return fbuf[pl.ds(pl.multiple_of(core * 64, 64), 64), :]

    def merge(k):
        for copy in to_sibling(k):
            copy.wait_recv()
        s1, s2 = s_own[k], s_sib[k]
        top = jnp.maximum(s1[0:4], s2[0:4])
        f1, f2 = jnp.exp2((s1[0:4] - top) * scale2), jnp.exp2((s2[0:4] - top) * scale2)
        s_mrg[k] = jnp.concatenate([top, s1[4:8] * f1 + s2[4:8] * f2], axis=0)
        f = factors(jnp.concatenate([f1, f2], axis=0))
        for b in range(BLK):
            o1 = o_own[k, core, :, b * 16 : b * 16 + 16, :].reshape(64, HD).astype(jnp.float32)
            o2 = o_sib[k, :, b * 16 : b * 16 + 16, :].reshape(64, HD).astype(jnp.float32)
            o = o1 * f[:, b : b + 1] + o2 * f[:, 4 + b : 5 + b]
            o_mrg[k, :, b * 16 : b * 16 + 16, :] = o.astype(jnp.bfloat16).reshape(4, 16, HD)

    def merge_and_send(j):
        k = (chip + 1 + j) % CHIPS
        merge(k)
        for copy in to_owner(k):
            copy.start()

    def step(j, carry):
        k = (chip + 1 + j) % CHIPS
        attend(k)
        for copy in to_sibling(k):
            copy.start()

        @pl.when(j > 0)
        def _():
            merge_and_send(j - 1)

        return carry

    lax.fori_loop(0, CHIPS, step, 0)
    merge(chip)
    o_fin[chip] = o_mrg[chip]
    s_fin[chip] = s_mrg[chip]

    key = heads[H + chip].astype(jnp.float32)
    val = heads[H + KVH + chip].astype(jnp.float32)
    old_key, old_val = pltpu.roll(key, 2, 0), pltpu.roll(val, 2, 0)
    is_later = (lax.broadcasted_iota(jnp.int32, (64, 1), 0) % ROWS) >= 2
    stats = jnp.zeros((64, 128), jnp.float32)
    lane64 = lax.broadcasted_iota(jnp.int32, (64, 128), 1)
    fresh = []
    for b in range(BLK):
        def wide(a):
            a = a[b * 16 : b * 16 + 16]
            return jnp.broadcast_to(a[None], (4, 16, HD)).reshape(64, HD)

        q = heads[pl.ds(me * 4, 4), b * 16 : b * 16 + 16, :].reshape(64, HD).astype(jnp.float32)
        own = jnp.sum(q * wide(key), axis=1, keepdims=True)
        prev = jnp.sum(q * wide(old_key), axis=1, keepdims=True)
        prev = jnp.where(is_later, prev, MASKED)
        top = jnp.maximum(own, prev)
        w0, w1 = jnp.exp2((own - top) * scale2), jnp.exp2((prev - top) * scale2)
        stats = jnp.where(lane64 == b, top, stats)
        stats = jnp.where(lane64 == BLK + b, w0 + w1, stats)
        w0 = w0.astype(jnp.bfloat16).astype(jnp.float32)
        w1 = w1.astype(jnp.bfloat16).astype(jnp.float32)
        fresh.append(w0 * wide(val) + w1 * wide(old_val))
    s_new = jnp.concatenate([stats, stats], axis=0).T[0:8]

    def wait_owner(j, carry):
        source = (chip + CHIPS - 1 - j) % CHIPS
        for copy in (
            pltpu.make_async_remote_copy(
                src_ref=o_mrg.at[source], dst_ref=o_fin.at[source],
                send_sem=fin_s.at[0, source], recv_sem=fin_r.at[0, source],
                device_id={"inst": sibling}, device_id_type=pl.DeviceIdType.MESH,
            ),
            pltpu.make_async_remote_copy(
                src_ref=s_mrg.at[source], dst_ref=s_fin.at[source],
                send_sem=fin_s.at[1, source], recv_sem=fin_r.at[1, source],
                device_id={"inst": sibling}, device_id_type=pl.DeviceIdType.MESH,
            ),
        ):
            copy.wait_recv()
        return carry

    lax.fori_loop(0, CHIPS - 1, wait_owner, 0)
    every = [s_fin[i] for i in range(CHIPS)] + [s_new]
    top = functools.reduce(jnp.maximum, [s[0:4] for s in every])
    shares = [jnp.exp2((s[0:4] - top) * scale2) for s in every]
    total = sum(s[4:8] * f for s, f in zip(every, shares))
    f = factors(jnp.concatenate([f / total for f in shares], axis=0))
    for b in range(BLK):
        o = fresh[b] * f[:, CHIPS * 4 + b : CHIPS * 4 + b + 1]
        for i in range(CHIPS):
            part = o_fin[i, :, b * 16 : b * 16 + 16, :].reshape(64, HD).astype(jnp.float32)
            o = o + part * f[:, i * 4 + b : i * 4 + b + 1]
        o = o.astype(jnp.bfloat16)
        for g in range(4):
            at = (g % 2) * HD
            att[me, g // 2, b * 16 : b * 16 + 16, at : at + HD] = o[g * 16 : g * 16 + 16]

    third = Gather([[lambda i, p=p: att.at[i, p]] for p in range(2)], g4s, g4r, me)
    for p in range(2):
        third.issue(p)
    loads[3].wait()
    loads[4].wait()
    oacc[...] = jnp.zeros_like(oacc)

    def use(i, p):
        at = pl.multiple_of(i * 512 + p * 256, 256)
        oacc[...] += dot_t(att[i, p], wo_v[:, pl.ds(at, 256)])

    third.drain(use=use)
    spread = (oacc[:, lowo:] * sel[:, :low]).astype(jnp.bfloat16)
    fin[...] = oacc[:, :lowo] + jnp.dot(spread, uo_ref[...], preferred_element_type=jnp.float32)
    for d in range(NI):
        piece = jnp.concatenate(
            [fin[pl.ds(4 * d, 4), i * 128 : (i + 1) * 128] for i in range(4)], axis=0
        )
        o_out[d] = piece.astype(jnp.bfloat16)
    r_out[me] = o_out[me]
    outs = []
    for j in range(1, NI):
        to = (me + j) % NI
        outs.append(send(o_out.at[to], r_out.at[me], os_sem.at[j], or_sem.at[j], to))
    for copy in outs:
        copy.wait_recv()
    out_ref[...] = r_out[...]

    def sent(j, carry):
        for copy in to_sibling(j):
            copy.wait_send()

        @pl.when(j != chip)
        def _():
            for copy in to_owner(j):
                copy.wait_send()

        return carry

    lax.fori_loop(0, CHIPS, sent, 0)
    for copy in outs:
        copy.wait_send()
    for gather in (first, second, third):
        gather.finish()


def one_kernel(slots, lens, adapter, tok, gain, freq, table, wq, wo, dq, do, uq, uo, pool):
    vm = pl.BlockSpec(memory_space=pltpu.VMEM)
    sm = pl.BlockSpec(memory_space=pltpu.SMEM)
    hbm = pl.BlockSpec(memory_space=pl.ANY)
    bf, f32 = jnp.bfloat16, jnp.float32
    qcols, ocols, low, width = wq.shape[0], wo.shape[0], dq.shape[0], wq.shape[1]
    V = pltpu.VMEM
    dma = pltpu.SemaphoreType.DMA
    return pl.pallas_call(
        block_kernel,
        out_shape=jax.ShapeDtypeStruct((NI, 16, 128), bf),
        in_specs=[sm, sm, sm, vm, vm, vm, vm, hbm, hbm, hbm, hbm, vm, vm, hbm],
        out_specs=vm,
        scratch_shapes=[
            V(pool.shape, bf),
            V((pool.shape[0] * 16, pool.shape[2]), bf),
            V((qcols + low, width), bf),
            V((ocols + low, width), bf),
            V((16, 2048), f32),
            V((NI * 16, 2048), bf),
            V((NI, 16, 128), f32),
            V((NI * 16, 256), f32),
            V((ALL, 256), f32),
            V((ALL, 128), f32),
            V((ALL, 128), f32),
            V((ALL, 128), f32),
            V((ALL, 128), f32),
            V((BLK, 16, TOK), f32),
            V((H + 2 * KVH, ALL, HD), bf),
            V((KVH, 2, 4, ALL, HD), bf),
            V((KVH, 8, 128), f32),
            V((KVH, 4, ALL, HD), bf),
            V((KVH, 8, 128), f32),
            V((KVH, 4, ALL, HD), bf),
            V((KVH, 8, 128), f32),
            V((KVH, 4, ALL, HD), bf),
            V((KVH, 8, 128), f32),
            V((128, 128), f32),
            V((NI, 2, ALL, 256), bf),
            V((ALL, ocols + low), f32),
            V((ALL, ocols), f32),
            V((NI, 16, 128), bf),
            V((NI, 16, 128), bf),
            dma((5,)),
            dma((3, NI)), dma((3, NI)),
            dma((3, NI)), dma((3, NI)),
            dma((2, KVH)), dma((2, KVH)),
            dma((2, KVH)), dma((2, KVH)),
            dma((2, NI)), dma((2, NI)),
            dma((NI,)), dma((NI,)),
        ],
        compiler_params=pltpu.CompilerParams(
            collective_id=0, has_side_effects=True, vmem_limit_bytes=58 * 1024 * 1024
        ),
        name="attention_block",
    )(slots, lens, adapter, tok, gain, freq, table, wq, wo, dq, do, uq, uo, pool)


def per_device_16(
    tokens, norm_gain, qkv_weight, out_weight, qkv_down, qkv_up, out_down, out_up,
    adapter_ids, cached_len, page_table, send_slots, kv_pool,
):
    steps, reqs, width = tokens.shape
    adapters, rank = qkv_down.shape[:2]
    low = adapters * rank
    rows = steps * reqs
    half = HD // 2
    freqs = np.float32(ROPE_BASE) ** (-(np.arange(half, dtype=np.float32) * 2.0) / HD)
    freqs = np.tile(freqs.astype(np.float32), 2).reshape(1, HD)
    out = one_kernel(
        send_slots, cached_len, adapter_ids, tokens, norm_gain.reshape(1, width),
        jnp.asarray(freqs), page_table, qkv_weight, out_weight,
        qkv_down.reshape(low, width), out_down.reshape(low, width),
        qkv_up.reshape(low, -1), out_up.reshape(low, -1), kv_pool,
    )
    out = out.reshape(NI, 4, rows, 128).transpose(2, 0, 1, 3)
    return out.reshape(steps, reqs, width)


def solution(mesh):
    in_specs = (
        P(None, ("dom", "inst"), None),
        P(),
        P("inst", None),
        P("inst", None),
        P(),
        P(None, None, "inst"),
        P(),
        P(None, None, "inst"),
        P(("dom", "inst")),
        P(("dom", "inst")),
        P(("dom", "inst"), None),
        P(("dom", "inst"), None),
        P(("dom", "inst"), None, None),
    )
    out_specs = P(None, ("dom", "inst"), None)
    n = mesh.shape["inst"]
    return jax.shard_map(
        per_device_16 if n == NI else functools.partial(per_device, n),
        mesh=mesh,
        in_specs=in_specs,
        out_specs=out_specs,
        check_vma=False,
    )
```

```python
import functools
import math

import jax
import jax.numpy as jnp
import numpy as np
from jax import lax
from jax.experimental import pallas as pl
from jax.experimental.pallas import tpu as pltpu
from jax.sharding import PartitionSpec as P

H = 64
KVH = 8
HD = 128
GROUPS = H // KVH
EXTRA = 128

EPSILON = 1e-05
ROPE_BASE = 500000.0
MASKED = -1e30


def rotate(vectors, position):
    half = vectors.shape[-1] // 2
    freqs = ROPE_BASE ** (-(jnp.arange(half, dtype=jnp.float32) * 2.0) / vectors.shape[-1])
    angle = position[:, None, None] * freqs
    cosine = jnp.cos(angle)
    sine = jnp.sin(angle)
    first = vectors[..., :half]
    second = vectors[..., half:]
    return jnp.concatenate(
        [first * cosine - second * sine, second * cosine + first * sine], axis=-1
    )


def normalize(hidden, norm_gain):
    values = hidden.astype(jnp.float32)
    factor = lax.rsqrt(jnp.mean(values * values, axis=-1, keepdims=True) + EPSILON)
    return (values * factor * norm_gain.astype(jnp.float32)).astype(jnp.bfloat16)


def expand(rows, down_maps, selector):
    every = jnp.einsum("rd,akd->rak", rows, down_maps, preferred_element_type=jnp.float32)
    chosen = jnp.sum(every * selector[:, :, None], axis=1).astype(jnp.bfloat16)
    spread = selector[:, :, None] * chosen[:, None, :].astype(jnp.float32)
    return spread.reshape(rows.shape[0], -1).astype(jnp.bfloat16)


def columns(gathered, spread, weight, up_maps):
    base = lax.dot_general(
        gathered, weight, (((1,), (1,)), ((), ())), preferred_element_type=jnp.float32
    )
    extra = jnp.dot(
        spread, up_maps.reshape(-1, up_maps.shape[2]), preferred_element_type=jnp.float32
    )
    return (base + extra).astype(jnp.bfloat16)


def page_codes(page_table, cached_len, page_len):
    reqs, maxp = page_table.shape
    begins = jnp.arange(maxp, dtype=jnp.int32) * page_len
    valid = jnp.clip(cached_len[:, None] - begins[None, :], 0, page_len)
    code = valid + 32 * jnp.arange(reqs, dtype=jnp.int32)[:, None]
    rows = jnp.arange(reqs * maxp, dtype=jnp.int32)
    match = page_table.reshape(-1)[:, None] == rows[None, :]
    return jnp.sum(jnp.where(match, code.reshape(-1)[:, None], 0), axis=0)


def per_device(
    n,
    tokens,
    norm_gain,
    qkv_weight,
    out_weight,
    qkv_down,
    qkv_up,
    out_down,
    out_up,
    adapter_ids,
    cached_len,
    page_table,
    send_slots,
    kv_pool,
):
    steps, reqs, width = tokens.shape
    adapters, rank = qkv_down.shape[:2]
    half_width = KVH * HD
    page_len = kv_pool.shape[1]
    pages = send_slots.shape[1]
    cap = pages // n
    rows = steps * reqs
    scale = 1.0 / math.sqrt(HD)
    me = lax.axis_index("inst")

    selector = (adapter_ids[:, None] == jnp.arange(adapters)[None, :]).astype(jnp.float32)
    selector = jnp.tile(selector, (steps, 1))
    normed = normalize(tokens, norm_gain).reshape(rows, width)
    spread = expand(normed, qkv_down, selector)
    codes = page_codes(page_table, cached_len, page_len)
    position = jnp.concatenate([cached_len + s for s in range(steps)])
    extra = jnp.concatenate(
        [
            spread,
            codes.reshape(rows, -1).astype(jnp.bfloat16),
            (position // 64).astype(jnp.bfloat16)[:, None],
            (position % 64).astype(jnp.bfloat16)[:, None],
        ],
        axis=1,
    )
    extra = jnp.pad(extra, ((0, 0), (0, EXTRA - extra.shape[1])))
    sent = jnp.concatenate([normed, extra], axis=1)
    everyone = lax.all_gather(sent, "inst", axis=0, tiled=True)
    low = adapters * rank
    per_row = pages // rows
    projected = columns(everyone[:, :width], everyone[:, width : width + low], qkv_weight, qkv_up)
    all_codes = everyone[:, width + low : width + low + per_row].astype(jnp.int32)
    my_codes = lax.dynamic_slice_in_dim(all_codes.reshape(n, pages), me * cap, cap, axis=1)
    spot = everyone[:, width + low + per_row : width + low + per_row + 2].astype(jnp.float32)
    all_position = spot[:, 0] * 64.0 + spot[:, 1]

    gathered = lax.all_gather(projected, "inst", axis=1, tiled=True)
    query = rotate(
        gathered[:, :width].astype(jnp.float32).reshape(n * rows, H, HD), all_position
    ).astype(jnp.bfloat16)
    query = query.reshape(n, rows, KVH, GROUPS, HD).transpose(0, 2, 1, 3, 4)
    query = query.reshape(n, KVH, rows * GROUPS, HD)

    slots = jnp.maximum(send_slots[0], 0)
    context = kv_pool[slots].reshape(n, cap * page_len, 2, KVH, HD)
    keys = context[:, :, 0]
    vals = context[:, :, 1]
    scores = (
        jnp.einsum("dkqf,dtkf->dkqt", query, keys, preferred_element_type=jnp.float32) * scale
    )
    within = jnp.arange(page_len)[None, None, :]
    valid = (within < (my_codes % 32)[:, :, None]).reshape(n, 1, cap * page_len)
    owner = jnp.broadcast_to((my_codes // 32)[:, :, None], (n, cap, page_len)).reshape(n, 1, -1)
    row_req = jnp.tile(jnp.repeat(jnp.arange(reqs), GROUPS), steps)[None, :, None]
    mask = (valid & (owner == row_req))[:, None]
    scores = jnp.where(mask, scores, MASKED)
    top = jnp.max(scores, axis=-1)
    weights = jnp.where(mask, jnp.exp(scores - top[..., None]), 0.0)
    total = jnp.sum(weights, axis=-1)
    mixed = jnp.einsum(
        "dkqt,dtkf->dkqf", weights.astype(jnp.bfloat16), vals, preferred_element_type=jnp.float32
    ).astype(jnp.bfloat16)
    stats = jnp.stack([top, total], axis=1)
    mixed = lax.all_to_all(mixed, "inst", split_axis=0, concat_axis=0, tiled=True)
    stats = lax.all_to_all(stats, "inst", split_axis=0, concat_axis=0, tiled=True)

    mine = lax.dynamic_slice_in_dim(gathered, me * rows, rows, axis=0)
    own_pos = position.astype(jnp.float32)
    own_query = lax.dynamic_index_in_dim(query, me, axis=0, keepdims=False)
    own_query = own_query.reshape(KVH, steps, reqs, GROUPS, HD)
    fresh_key = rotate(
        mine[:, width : width + half_width].astype(jnp.float32).reshape(rows, KVH, HD), own_pos
    ).astype(jnp.bfloat16)
    fresh_key = fresh_key.reshape(steps, reqs, KVH, HD)
    fresh_val = mine[:, width + half_width :].reshape(steps, reqs, KVH, HD)
    new_scores = (
        jnp.einsum("ksrgf,nrkf->ksrgn", own_query, fresh_key, preferred_element_type=jnp.float32)
        * scale
    )
    seen = jnp.arange(steps)[None, :] <= jnp.arange(steps)[:, None]
    seen = seen[None, :, None, None, :]
    new_scores = jnp.where(seen, new_scores, MASKED)
    tops = stats[:, 0].reshape(n, KVH, steps, reqs, GROUPS)
    totals = stats[:, 1].reshape(n, KVH, steps, reqs, GROUPS)
    best = jnp.maximum(jnp.max(tops, axis=0), jnp.max(new_scores, axis=-1))
    factors = jnp.exp(tops - best[None])
    new_weights = jnp.where(seen, jnp.exp(new_scores - best[..., None]), 0.0)
    total = jnp.sum(factors * totals, axis=0) + jnp.sum(new_weights, axis=-1)
    mixed = mixed.reshape(n, KVH, steps, reqs, GROUPS, HD).astype(jnp.float32)
    summed = jnp.sum(mixed * factors[..., None], axis=0)
    summed = summed + jnp.einsum(
        "ksrgn,nrkf->ksrgf",
        new_weights.astype(jnp.bfloat16),
        fresh_val,
        preferred_element_type=jnp.float32,
    )
    attended = (summed / total[..., None]).transpose(1, 2, 0, 3, 4)
    attended = attended.reshape(rows, width).astype(jnp.bfloat16)
    low_out = expand(attended, out_down, selector)
    both = jnp.concatenate([attended, jnp.pad(low_out, ((0, 0), (0, EXTRA - low)))], axis=1)
    every_att = lax.all_gather(both, "inst", axis=0, tiled=True)
    out_cols = columns(every_att[:, :width], every_att[:, width : width + low], out_weight, out_up)
    result = lax.all_to_all(out_cols, "inst", split_axis=0, concat_axis=1, tiled=True)
    return result.reshape(steps, reqs, width)


NZ, NY, NC = 4, 2, 2
NI = NZ * NY * NC
CHIPS = NZ * NY
ROWS = 4
ALL = NI * ROWS
BLK = 4
TOK = 512
KC = 4
FLOOR = -1e29


def send(src, dst, send_sem, recv_sem, to):
    copy = pltpu.make_async_remote_copy(
        src_ref=src,
        dst_ref=dst,
        send_sem=send_sem,
        recv_sem=recv_sem,
        device_id={"inst": to},
        device_id_type=pl.DeviceIdType.MESH,
    )
    copy.start()
    return copy


def index_of(z, y, c):
    return (z * NY + y) * NC + c


class Gather:
    def __init__(self, pieces, send_sems, recv_sems, me):
        self.pieces, self.send_sems, self.recv_sems, self.me = pieces, send_sems, recv_sems, me
        self.z, self.y, self.c = me // (NY * NC), (me // NC) % NY, me % NC
        self.first = [sum(len(q) for q in pieces[:p]) for p in range(len(pieces))]
        self.slots = [0] * len(pieces)
        self.started = []

    def put(self, p, block, to):
        slot = self.slots[p]
        self.slots[p] += 1
        for v, view in enumerate(self.pieces[p], self.first[p]):
            self.started.append(
                send(view(block), view(block), self.send_sems.at[v, slot],
                     self.recv_sems.at[v, block], to)
            )

    def arrive(self, p, block):
        for v, view in enumerate(self.pieces[p], self.first[p]):
            pltpu.make_async_remote_copy(
                src_ref=view(block),
                dst_ref=view(block),
                send_sem=self.send_sems.at[v, 0],
                recv_sem=self.recv_sems.at[v, block],
                device_id={"inst": self.me},
                device_id_type=pl.DeviceIdType.MESH,
            ).wait_recv()

    def issue(self, p):
        z, y, c = self.z, self.y, self.c
        for j in range(1, NZ):
            self.put(p, self.me, index_of((z + j) % NZ, y, c))
        self.put(p, self.me, index_of(z, 1 - y, c))
        self.put(p, self.me, index_of(z, y, 1 - c))

    def drain(self, use=None, fillers=()):
        z, y, c = self.z, self.y, self.c
        fillers = list(fillers)
        pending = []

        def idle():
            if pending:
                use(*pending.pop(0))
            elif fillers:
                fillers.pop(0)()

        def done(p, block):
            if use is not None:
                pending.append((block, p))
            idle()

        def from_z(p):
            for j in range(1, NZ):
                block = index_of((z + NZ - j) % NZ, y, c)
                self.arrive(p, block)
                self.put(p, block, index_of(z, 1 - y, c))
                self.put(p, block, index_of(z, y, 1 - c))
                done(p, block)

        def from_y(p):
            for j in range(NZ):
                block = index_of((z + NZ - j) % NZ, 1 - y, c)
                self.arrive(p, block)
                self.put(p, block, index_of(z, y, 1 - c))
                done(p, block)

        count = len(self.pieces)
        if use is not None:
            pending.extend((self.me, p) for p in range(count))
        idle()
        for p in range(count):
            from_z(p)
            if p > 0:
                from_y(p - 1)
        from_y(count - 1)
        for p in range(count):
            for yy in (y, 1 - y):
                for j in range(NZ):
                    block = index_of((z + NZ - j) % NZ, yy, 1 - c)
                    self.arrive(p, block)
                    done(p, block)
        while pending or fillers:
            idle()

    def finish(self):
        for copy in self.started:
            copy.wait_send()


def dot_t(a, b):
    return lax.dot_general(a, b, (((1,), (1,)), ((), ())), preferred_element_type=jnp.float32)


def block_kernel(
    slots_ref, len_ref, adapter_ref, tok_ref, gain_ref, freq_ref, table_ref, wq_ref, wo_ref, dq_ref, do_ref, uq_ref, uo_ref, pool_ref,
    out_ref,
    pool_v, ctx, wq_v, wo_v, x_f, x_all, meta_all, acc, proj, cc, ss, sel, nvr, bias, heads,
    o_own, s_own, o_sib, s_sib, o_mrg, s_mrg, o_y, s_y, o_two, s_two, o_fin, s_fin, fbuf, att, oacc, fin, o_out, r_out,
    local_sem, g1s, g1r, g2s, g2r, sib_s, sib_r, y_s, y_r, fin_s, fin_r, g4s, g4r, os_sem, or_sem,
):
    me = lax.axis_index("inst")
    chip, core = me // NC, me % NC
    sibling = chip * NC + 1 - core
    scale2 = math.log2(math.e) / math.sqrt(HD)
    lowq, lowo = wq_ref.shape[0], wo_ref.shape[0]
    low = dq_ref.shape[0]

    loads = [
        pltpu.make_async_copy(pool_ref, pool_v, local_sem.at[0]),
        pltpu.make_async_copy(wq_ref, wq_v.at[pl.ds(0, lowq)], local_sem.at[1]),
        pltpu.make_async_copy(dq_ref, wq_v.at[pl.ds(lowq, low)], local_sem.at[2]),
        pltpu.make_async_copy(wo_ref, wo_v.at[pl.ds(0, lowo)], local_sem.at[3]),
        pltpu.make_async_copy(do_ref, wo_v.at[pl.ds(lowo, low)], local_sem.at[4]),
    ]
    for load in loads:
        load.start()

    barrier = pltpu.get_barrier_semaphore()
    for j in range(1, NI):
        pl.semaphore_signal(
            barrier, inc=1, device_id={"inst": (me + j) % NI},
            device_id_type=pl.DeviceIdType.MESH,
        )
    gain = gain_ref[...].astype(jnp.float32)
    for s in range(2):
        values = tok_ref[s].astype(jnp.float32)
        mean = jnp.sum(values * values, axis=-1, keepdims=True) / values.shape[-1]
        values = values * lax.rsqrt(mean + EPSILON) * gain
        for kc in range(KC):
            x_f[pl.ds(kc * 4 + 2 * s, 2), :] = values[:, kc * 2048 : (kc + 1) * 2048]
    x_all[pl.ds(pl.multiple_of(me * 16, 16), 16), :] = x_f[...].astype(jnp.bfloat16)
    lane = lax.broadcasted_iota(jnp.int32, (128, 128), 1)
    sub = lax.broadcasted_iota(jnp.int32, (128, 128), 0)
    row8 = lax.broadcasted_iota(jnp.int32, (8, 128), 0)
    lane8 = lax.broadcasted_iota(jnp.int32, (8, 128), 1)
    req8 = row8 % 2
    length = jnp.where(req8 == 0, len_ref[0], len_ref[1])
    position = (length + (row8 // 2) % 2).astype(jnp.float32)
    angle = position * freq_ref[...]
    sine = jnp.sin(angle)
    sine = jnp.where(lane8 < HD // 2, -sine, sine)
    meta_all[me, pl.ds(0, 8), :] = jnp.where(row8 < 4, jnp.cos(angle), sine)
    counts = jnp.zeros((128, 128), jnp.float32)
    maxp = table_ref.shape[1]
    begin = lax.broadcasted_iota(jnp.int32, (1, maxp), 1) * 16
    for r in range(2):
        valid = jnp.clip(len_ref[r] - begin, 0, 16).astype(jnp.float32)
        hit = jnp.broadcast_to(table_ref[r : r + 1, :], (128, maxp)) == sub[:, :maxp]
        column = jnp.sum(jnp.where(hit, valid, 0.0), axis=1, keepdims=True)
        counts = jnp.where(lane == r, column, counts)
    adapter = jnp.where(req8 == 0, adapter_ref[0], adapter_ref[1])
    chosen = jnp.where(lane8 // 16 == adapter, 1.0, 0.0)
    meta_all[me, pl.ds(8, 8), :] = jnp.where(row8 < 4, counts.T[0:8], chosen)
    pl.semaphore_wait(barrier, NI - 1)

    def x_view(p):
        return lambda i: x_all.at[
            pl.ds(pl.multiple_of(i * 16, 16), 16), pl.ds(p * 1024, 1024)
        ]

    first = Gather([[x_view(0)], [x_view(1), lambda i: meta_all.at[i]]], g1s, g1r, me)
    for p in range(2):
        first.issue(p)
    first.drain()
    for d in range(NI):
        cc[pl.ds(4 * d, 4), :] = meta_all[d, 0:4, :]
        ss[pl.ds(4 * d, 4), :] = meta_all[d, 4:8, :]
        sel[pl.ds(4 * d, 4), :] = meta_all[d, 12:16, :]
        nvr[pl.ds(4 * d, 2), :] = meta_all[d, 8:10, :]
        nvr[pl.ds(4 * d + 2, 2), :] = meta_all[d, 8:10, :]
    pick = jnp.where(sub == me * 8 + lane // 16, 1.0, 0.0)
    nvx = jnp.dot(nvr[...], pick, preferred_element_type=jnp.float32)

    row16 = lax.broadcasted_iota(jnp.int32, (16, 128), 0) // ROWS
    tok16 = (lax.broadcasted_iota(jnp.int32, (16, 128), 1) % 16).astype(jnp.float32)
    for b in range(BLK):
        shown = jnp.where(tok16 < nvx[b * 16 : b * 16 + 16], 0.0, MASKED)
        for d in range(4):
            bias[b, :, d * 128 : (d + 1) * 128] = jnp.where(row16 == d, shown, MASKED)

    loads[1].wait()
    loads[2].wait()
    row_chunk = (lax.broadcasted_iota(jnp.int32, (NI * 16, 1), 0) // ROWS) % KC
    own_heads = lowq // HD
    tiles = [(4, 1), (0, 2), (2, 2)]
    second = Gather(
        [
            [lambda i, at=at, n=n: heads.at[pl.ds(i * own_heads + at, n)]]
            for at, n in tiles
        ],
        g2s, g2r, me,
    )
    spread = None
    for p, (head_at, count) in enumerate(tiles):
        begin = head_at * HD
        size = count * HD + (low if p == 0 else 0)

        def chunk(kc, carry, begin=begin, size=size):
            at = pl.multiple_of(kc * 2048, 2048)
            part = dot_t(x_all[...], wq_v[pl.ds(begin, size), pl.ds(at, 2048)])
            acc[:, :size] = jnp.where(row_chunk == kc, part, acc[:, :size])
            return carry

        lax.fori_loop(0, KC, chunk, 0)
        for d in range(NI):
            piece = acc[16 * d : 16 * d + 8, :size] + acc[16 * d + 8 : 16 * d + 16, :size]
            proj[pl.ds(4 * d, 4), :size] = piece[0:4] + piece[4:8]
        if p == 0:
            spread = (proj[:, HD : HD + low] * sel[:, :low]).astype(jnp.bfloat16)
        extra = jnp.dot(
            spread, uq_ref[:, begin : begin + count * HD], preferred_element_type=jnp.float32
        )
        for i in range(count):
            part = proj[:, i * HD : (i + 1) * HD] + extra[:, i * HD : (i + 1) * HD]
            part = part.astype(jnp.bfloat16).astype(jnp.float32)
            turned = part * cc[...] + pltpu.roll(part, HD // 2, 1) * ss[...]
            head = me * own_heads + head_at + i
            heads[head] = jnp.where(head < H + KVH, turned, part).astype(jnp.bfloat16)
        second.issue(p)

    loads[0].wait()

    def page(i, carry):
        slot = jnp.maximum(slots_ref[0, i], 0)
        ctx[pl.ds(pl.multiple_of(i * 16, 16), 16), :] = pool_v[slot]
        return carry

    pages = pool_ref.shape[0]
    second.drain(
        fillers=[
            lambda q=q: lax.fori_loop(q * pages // 8, (q + 1) * pages // 8, page, 0)
            for q in range(8)
        ]
    )

    def attend(k):
        stats = jnp.zeros((128, 128), jnp.float32)
        for b in range(BLK):
            q = heads[pl.ds(k * GROUPS, GROUPS), b * 16 : b * 16 + 16, :].reshape(128, HD)
            keys = ctx[b * TOK : (b + 1) * TOK, pl.ds(pl.multiple_of(k * HD, HD), HD)]
            vals = ctx[
                b * TOK : (b + 1) * TOK, pl.ds(pl.multiple_of((KVH + k) * HD, HD), HD)
            ]
            s = dot_t(q, keys).reshape(GROUPS, 16, TOK) + bias[b][None]
            s = s.reshape(128, TOK)
            top = jnp.maximum(jnp.max(s, axis=1, keepdims=True), FLOOR)
            p = jnp.exp2((s - top) * scale2)
            count = jnp.sum(p, axis=1, keepdims=True)
            o = jnp.dot(p.astype(jnp.bfloat16), vals, preferred_element_type=jnp.float32)
            o = o.astype(jnp.bfloat16).reshape(2, 4, 16, HD)
            o_own[k, :, :, b * 16 : b * 16 + 16, :] = o
            stats = jnp.where(lane == b, top, stats)
            stats = jnp.where(lane == BLK + b, count, stats)
        s_own[k] = stats.T[0:8]

    def to_sibling(k):
        return (
            pltpu.make_async_remote_copy(
                src_ref=o_own.at[k, 1 - core], dst_ref=o_sib.at[k],
                send_sem=sib_s.at[0, k], recv_sem=sib_r.at[0, k],
                device_id={"inst": sibling}, device_id_type=pl.DeviceIdType.MESH,
            ),
            pltpu.make_async_remote_copy(
                src_ref=s_own.at[k], dst_ref=s_sib.at[k],
                send_sem=sib_s.at[1, k], recv_sem=sib_r.at[1, k],
                device_id={"inst": sibling}, device_id_type=pl.DeviceIdType.MESH,
            ),
        )

    z, y = chip // NY, chip % NY

    def target(j):
        return ((z + 1 + j // 2) % NZ) * NY + (1 - y + (2 * y - 1) * (j % 2))

    def copies(srcs, dsts, ss, rs, at_s, at_r, to):
        return tuple(
            pltpu.make_async_remote_copy(
                src_ref=a, dst_ref=b, send_sem=ss.at[i, at_s], recv_sem=rs.at[i, at_r],
                device_id={"inst": to}, device_id_type=pl.DeviceIdType.MESH,
            )
            for i, (a, b) in enumerate(zip(srcs, dsts))
        )

    def across_y(t):
        k = target(2 * t)
        return copies(
            (o_mrg.at[k], s_mrg.at[k]), (o_y.at[t], s_y.at[t]), y_s, y_r, t, t,
            index_of(z, 1 - y, core),
        )

    def to_owner(t):
        return copies(
            (o_two.at[t], s_two.at[t]), (o_fin.at[z], s_fin.at[z]), fin_s, fin_r, t, z,
            index_of((z + 1 + t) % NZ, y, core),
        )

    def factors(rows):
        pad = jnp.zeros((128 - rows.shape[0], 128), jnp.float32)
        fbuf[...] = jnp.concatenate([rows, pad], axis=0).T
        return fbuf[pl.ds(pl.multiple_of(core * 64, 64), 64), :]

    def combine(o1, s1, o2, s2, o_to, s_to):
        top = jnp.maximum(s1[0:4], s2[0:4])
        f1, f2 = jnp.exp2((s1[0:4] - top) * scale2), jnp.exp2((s2[0:4] - top) * scale2)
        s_to[...] = jnp.concatenate([top, s1[4:8] * f1 + s2[4:8] * f2], axis=0)
        f = factors(jnp.concatenate([f1, f2], axis=0))
        for b in range(BLK):
            at = slice(b * 16, b * 16 + 16)
            a = o1[:, at, :].reshape(64, HD).astype(jnp.float32)
            e = o2[:, at, :].reshape(64, HD).astype(jnp.float32)
            o = a * f[:, b : b + 1] + e * f[:, 4 + b : 5 + b]
            o_to[:, at, :] = o.astype(jnp.bfloat16).reshape(4, 16, HD)

    def merge_core(j):
        k = target(j)
        for copy in to_sibling(k):
            copy.wait_recv()
        combine(
            o_own.at[k, core], s_own[k], o_sib.at[k], s_sib[k], o_mrg.at[k], s_mrg.at[k]
        )

    def merge_y(t, o_to, s_to):
        k = target(2 * t + 1)
        for copy in across_y(t):
            copy.wait_recv()
        combine(o_mrg.at[k], s_mrg[k], o_y.at[t], s_y[t], o_to, s_to)

    def step(j, carry):
        k = target(j)
        attend(k)
        for copy in to_sibling(k):
            copy.start()

        @pl.when(j > 0)
        def _():
            merge_core(j - 1)

        @pl.when(j % 2 == 1)
        def _():
            for copy in across_y(j // 2):
                copy.start()

        @pl.when((j >= 3) & (j % 2 == 1))
        def _():
            t = j // 2 - 1
            merge_y(t, o_two.at[t], s_two.at[t])
            for copy in to_owner(t):
                copy.start()

        return carry

    lax.fori_loop(0, CHIPS, step, 0)
    merge_core(CHIPS - 1)
    merge_y(NZ - 1, o_fin.at[z], s_fin.at[z])

    key = heads[H + chip].astype(jnp.float32)
    val = heads[H + KVH + chip].astype(jnp.float32)
    old_key, old_val = pltpu.roll(key, 2, 0), pltpu.roll(val, 2, 0)
    is_later = (lax.broadcasted_iota(jnp.int32, (64, 1), 0) % ROWS) >= 2
    stats = jnp.zeros((64, 128), jnp.float32)
    lane64 = lax.broadcasted_iota(jnp.int32, (64, 128), 1)
    fresh = []
    for b in range(BLK):
        def wide(a):
            a = a[b * 16 : b * 16 + 16]
            return jnp.broadcast_to(a[None], (4, 16, HD)).reshape(64, HD)

        q = heads[pl.ds(me * 4, 4), b * 16 : b * 16 + 16, :].reshape(64, HD).astype(jnp.float32)
        own = jnp.sum(q * wide(key), axis=1, keepdims=True)
        prev = jnp.sum(q * wide(old_key), axis=1, keepdims=True)
        prev = jnp.where(is_later, prev, MASKED)
        top = jnp.maximum(own, prev)
        w0, w1 = jnp.exp2((own - top) * scale2), jnp.exp2((prev - top) * scale2)
        stats = jnp.where(lane64 == b, top, stats)
        stats = jnp.where(lane64 == BLK + b, w0 + w1, stats)
        w0 = w0.astype(jnp.bfloat16).astype(jnp.float32)
        w1 = w1.astype(jnp.bfloat16).astype(jnp.float32)
        fresh.append(w0 * wide(val) + w1 * wide(old_val))
    s_new = jnp.concatenate([stats, stats], axis=0).T[0:8]

    for t in range(NZ - 1):
        source = (z + NZ - 1 - t) % NZ
        for copy in copies(
            (o_two.at[t], s_two.at[t]), (o_fin.at[source], s_fin.at[source]),
            fin_s, fin_r, t, source, sibling,
        ):
            copy.wait_recv()
    every = [s_fin[i] for i in range(NZ)] + [s_new]
    top = functools.reduce(jnp.maximum, [s[0:4] for s in every])
    shares = [jnp.exp2((s[0:4] - top) * scale2) for s in every]
    total = sum(s[4:8] * f for s, f in zip(every, shares))
    f = factors(jnp.concatenate([f / total for f in shares], axis=0))
    for b in range(BLK):
        o = fresh[b] * f[:, NZ * 4 + b : NZ * 4 + b + 1]
        for i in range(NZ):
            part = o_fin[i, :, b * 16 : b * 16 + 16, :].reshape(64, HD).astype(jnp.float32)
            o = o + part * f[:, i * 4 + b : i * 4 + b + 1]
        o = o.astype(jnp.bfloat16)
        for g in range(4):
            at = (g % 2) * HD
            att[me, g // 2, b * 16 : b * 16 + 16, at : at + HD] = o[g * 16 : g * 16 + 16]

    third = Gather([[lambda i, p=p: att.at[i, p]] for p in range(2)], g4s, g4r, me)
    for p in range(2):
        third.issue(p)
    loads[3].wait()
    loads[4].wait()
    oacc[...] = jnp.zeros_like(oacc)

    def use(i, p):
        at = pl.multiple_of(i * 512 + p * 256, 256)
        oacc[...] += dot_t(att[i, p], wo_v[:, pl.ds(at, 256)])

    third.drain(use=use)
    spread = (oacc[:, lowo:] * sel[:, :low]).astype(jnp.bfloat16)
    fin[...] = oacc[:, :lowo] + jnp.dot(spread, uo_ref[...], preferred_element_type=jnp.float32)
    for d in range(NI):
        piece = jnp.concatenate(
            [fin[pl.ds(4 * d, 4), i * 128 : (i + 1) * 128] for i in range(4)], axis=0
        )
        o_out[d] = piece.astype(jnp.bfloat16)
    r_out[me] = o_out[me]
    outs = []
    for j in range(1, NI):
        to = (me + j) % NI
        outs.append(send(o_out.at[to], r_out.at[me], os_sem.at[j], or_sem.at[j], to))
    for copy in outs:
        copy.wait_recv()
    out_ref[...] = r_out[...]

    def sent(j, carry):
        for copy in to_sibling(j):
            copy.wait_send()
        return carry

    lax.fori_loop(0, CHIPS, sent, 0)
    for t in range(NZ):
        for copy in across_y(t) + (to_owner(t) if t < NZ - 1 else ()):
            copy.wait_send()
    for copy in outs:
        copy.wait_send()
    for gather in (first, second, third):
        gather.finish()


def one_kernel(slots, lens, adapter, tok, gain, freq, table, wq, wo, dq, do, uq, uo, pool):
    vm = pl.BlockSpec(memory_space=pltpu.VMEM)
    sm = pl.BlockSpec(memory_space=pltpu.SMEM)
    hbm = pl.BlockSpec(memory_space=pl.ANY)
    bf, f32 = jnp.bfloat16, jnp.float32
    qcols, ocols, low, width = wq.shape[0], wo.shape[0], dq.shape[0], wq.shape[1]
    V = pltpu.VMEM
    dma = pltpu.SemaphoreType.DMA
    return pl.pallas_call(
        block_kernel,
        out_shape=jax.ShapeDtypeStruct((NI, 16, 128), bf),
        in_specs=[sm, sm, sm, vm, vm, vm, vm, hbm, hbm, hbm, hbm, vm, vm, hbm],
        out_specs=vm,
        scratch_shapes=[
            V(pool.shape, bf),
            V((pool.shape[0] * 16, pool.shape[2]), bf),
            V((qcols + low, width), bf),
            V((ocols + low, width), bf),
            V((16, 2048), f32),
            V((NI * 16, 2048), bf),
            V((NI, 16, 128), f32),
            V((NI * 16, 256), f32),
            V((ALL, 256), f32),
            V((ALL, 128), f32),
            V((ALL, 128), f32),
            V((ALL, 128), f32),
            V((ALL, 128), f32),
            V((BLK, 16, TOK), f32),
            V((H + 2 * KVH, ALL, HD), bf),
            V((KVH, 2, 4, ALL, HD), bf),
            V((KVH, 8, 128), f32),
            V((KVH, 4, ALL, HD), bf),
            V((KVH, 8, 128), f32),
            V((KVH, 4, ALL, HD), bf),
            V((KVH, 8, 128), f32),
            V((NZ, 4, ALL, HD), bf),
            V((NZ, 8, 128), f32),
            V((NZ, 4, ALL, HD), bf),
            V((NZ, 8, 128), f32),
            V((NZ, 4, ALL, HD), bf),
            V((NZ, 8, 128), f32),
            V((128, 128), f32),
            V((NI, 2, ALL, 256), bf),
            V((ALL, ocols + low), f32),
            V((ALL, ocols), f32),
            V((NI, 16, 128), bf),
            V((NI, 16, 128), bf),
            dma((5,)),
            dma((3, NI)), dma((3, NI)),
            dma((3, NI)), dma((3, NI)),
            dma((2, KVH)), dma((2, KVH)),
            dma((2, NZ)), dma((2, NZ)),
            dma((2, NZ)), dma((2, NZ)),
            dma((2, NI)), dma((2, NI)),
            dma((NI,)), dma((NI,)),
        ],
        compiler_params=pltpu.CompilerParams(
            collective_id=0, has_side_effects=True, vmem_limit_bytes=58 * 1024 * 1024
        ),
        name="attention_block",
    )(slots, lens, adapter, tok, gain, freq, table, wq, wo, dq, do, uq, uo, pool)


def per_device_16(
    tokens, norm_gain, qkv_weight, out_weight, qkv_down, qkv_up, out_down, out_up,
    adapter_ids, cached_len, page_table, send_slots, kv_pool,
):
    steps, reqs, width = tokens.shape
    adapters, rank = qkv_down.shape[:2]
    low = adapters * rank
    rows = steps * reqs
    half = HD // 2
    freqs = np.float32(ROPE_BASE) ** (-(np.arange(half, dtype=np.float32) * 2.0) / HD)
    freqs = np.tile(freqs.astype(np.float32), 2).reshape(1, HD)
    out = one_kernel(
        send_slots, cached_len, adapter_ids, tokens, norm_gain.reshape(1, width),
        jnp.asarray(freqs), page_table, qkv_weight, out_weight,
        qkv_down.reshape(low, width), out_down.reshape(low, width),
        qkv_up.reshape(low, -1), out_up.reshape(low, -1), kv_pool,
    )
    out = out.reshape(NI, 4, rows, 128).transpose(2, 0, 1, 3)
    return out.reshape(steps, reqs, width)


def solution(mesh):
    in_specs = (
        P(None, ("dom", "inst"), None),
        P(),
        P("inst", None),
        P("inst", None),
        P(),
        P(None, None, "inst"),
        P(),
        P(None, None, "inst"),
        P(("dom", "inst")),
        P(("dom", "inst")),
        P(("dom", "inst"), None),
        P(("dom", "inst"), None),
        P(("dom", "inst"), None, None),
    )
    out_specs = P(None, ("dom", "inst"), None)
    n = mesh.shape["inst"]
    return jax.shard_map(
        per_device_16 if n == NI else functools.partial(per_device, n),
        mesh=mesh,
        in_specs=in_specs,
        out_specs=out_specs,
        check_vma=False,
    )
```
